32 devices in a mesh: layer: 8 (over z, x), ctx: 4 (over y, core).
Axes of the slice: x: 2, y: 2, z: 4, core: 2. Of those that a mesh axis runs over, the one named last changes fastest.
Arguments:
- queries: bfloat16 [8, 512, 1536], P('layer', 'ctx'), may hold values from -9 to 9
- keys: bfloat16 [512, 512], P(('ctx', 'layer')), may hold values from -4 to 4
- values: bfloat16 [512, 512], P(('ctx', 'layer')), may hold values from -6 to 6
- head: float32 [8, 1536, 2], P('layer'), may hold values from -1.5 to 1.5
- segments: int32 [512], replicated, may hold values from 0 to 4, as said below
- label_mask: int32 [512], P('ctx'), may hold values 0 or 1
- labels: int32 [512], P('ctx'), may hold values from 0 to 1
Outputs:
- loss: float32 [8], P('layer')
- query_gradient: float32 [8, 512, 1536], P('layer', 'ctx')
- grad_keys: float32 [512, 512], P(('ctx', 'layer'))
- grad_values: float32 [512, 512], P(('ctx', 'layer'))
- head_gradient_rows: float32 [8, 1536, 2], P('layer')
The draws below stay inside these ranges and needn't reach their ends.
Inputs may be any that keep to these rules, and one draw needn't show every extreme that they name: `segments`: document ids never fall; the first document spans exactly 384 positions and the positions after it form exactly four more documents, each of one position or more.
All inputs are finite; a program needn't handle non-finite values. No bound on the sum of `label_mask` on one device may be relied on, other than what follows from the above.
Results may differ from the reference program's by a relative error of at most 0.019.
Values may be sent and summed in bfloat16 or wider, within the bound.
A program may use at most 128 MiB of HBM per device.

```python
import jax
import jax.numpy as jnp
from jax import lax

QUERY_HEADS = 12
KEY_VALUE_HEADS = 4
HEAD_WIDTH = 128
CLASSES = 2
LOCAL_TOKENS = 128
TOKEN_COUNT = 512
LAYERS = 8
DOC_MOST = 384
N_CTX = 4


rest_cuts = 3


def doc_ids(key):
    base_offset = jax.random.fold_in(key, 11)
    rest_rows = TOKEN_COUNT - DOC_MOST
    order = jax.random.permutation(base_offset, rest_rows - 1)
    cuts = order[:rest_cuts].astype(jnp.int32) + 1
    positions = jnp.arange(TOKEN_COUNT, dtype=jnp.int32)
    offset_rows = positions - DOC_MOST
    later = 1 + jnp.sum((cuts[None, :] <= offset_rows[:, None]).astype(jnp.int32), axis=1)
    return jnp.where(positions < DOC_MOST, 0, later).astype(jnp.int32)


def draw_segments(key, part):
    return doc_ids(key)


def draw_keys(key, part):
    row_count = jnp.clip(jax.random.normal(jax.random.fold_in(key, 41), (TOKEN_COUNT, KEY_VALUE_HEADS * HEAD_WIDTH), jnp.float32), -4.0, 4.0)
    return row_count.astype(jnp.bfloat16)


def draw_queries(key, part):
    row_count = jnp.clip(jax.random.normal(jax.random.fold_in(key, 51), (LAYERS, TOKEN_COUNT, QUERY_HEADS * HEAD_WIDTH), jnp.float32), -4.0, 4.0)
    return row_count.astype(jnp.bfloat16)


def with_ends(entries, rng, least, high):
    longest = entries.shape.index(max(entries.shape))
    spots = []
    for shift in (0, 1):
        where = [jax.random.randint(jax.random.fold_in(rng, axis), (), 0, length) for axis, length in enumerate(entries.shape)]
        where[longest] = (where[longest] + shift) % entries.shape[longest]
        spots.append(tuple(where))
    return entries.at[spots[0]].set(least).at[spots[1]].set(high)


def level_of(key, shape, shards, low, largest):
    def one(position, shards_of):
        draws = jax.random.uniform(jax.random.fold_in(jax.random.fold_in(key, 6), position), (shards_of,), jnp.float32, low / len(shards), largest / len(shards))
        return jnp.repeat(jnp.exp(draws), shape[position] // shards_of).reshape((-1,) + (1,) * (len(shape) - position - 1))

    loudness = one(*shards[0])
    for cut in shards[1:]:
        loudness = loudness * one(*cut)
    return loudness


def bell_draw(own_key, dims, scale, reach, split=(), held_as=jnp.bfloat16):
    loudness = level_of(own_key, dims, split, -0.22, 0.18) if split else 1.0
    result = jax.random.normal(own_key, dims, jnp.float32) * scale * loudness
    return jnp.minimum(jnp.maximum(result, -reach), reach).astype(held_as)


def setup_inputs(seed: int = 0) -> dict:
    splits = jax.random.split(jax.random.key(seed), 8)
    queries = draw_queries(jax.random.fold_in(splits[7], 71), 0)
    keys = draw_keys(jax.random.fold_in(splits[7], 71), 0)
    values = bell_draw(splits[2], (TOKEN_COUNT, KEY_VALUE_HEADS * HEAD_WIDTH), 1.0, 6.0, ((0, 32),))
    head = bell_draw(splits[3], (LAYERS, QUERY_HEADS * HEAD_WIDTH, CLASSES), 0.25, 1.5, ((0, 8),), jnp.float32)
    segments = draw_segments(jax.random.fold_in(splits[7], 71), 0)
    label_mask = with_ends((jax.random.randint(splits[5], (TOKEN_COUNT,), 0, 2) < 1).astype(jnp.int32), jax.random.fold_in(splits[5], 1), 0, 1)
    labels = with_ends(jax.random.randint(splits[6], (TOKEN_COUNT,), 0, CLASSES), jax.random.fold_in(splits[6], 1), 0, CLASSES - 1).astype(jnp.int32)
    return {"queries": queries, "keys": keys, "values": values, "head": head, "segments": segments, "label_mask": label_mask, "labels": labels}


NEGATIVE_FILL = -1.0e30
HIGH = lax.Precision.HIGHEST


def masked_scores(query_tensor_four, key_tensor_three, seg_q, seg_k, q_start, k_start):
    s = jnp.einsum("tgrd,ngd->tgrn", query_tensor_four.astype(jnp.float32), key_tensor_three.astype(jnp.float32), precision=HIGH) * (HEAD_WIDTH ** -0.5)
    q_pos = q_start + jnp.arange(query_tensor_four.shape[0], dtype=jnp.int32)
    k_pos = k_start + jnp.arange(key_tensor_three.shape[0], dtype=jnp.int32)
    allowed = (k_pos[None, :] <= q_pos[:, None]) & (seg_k[None, :] == seg_q[:, None])
    return jnp.where(allowed[:, None, None, :], s, NEGATIVE_FILL)


def reference(queries, keys, values, head, segments, label_mask, labels):
    head_group = QUERY_HEADS // KEY_VALUE_HEADS
    key_tensor_three = keys.reshape(TOKEN_COUNT, KEY_VALUE_HEADS, HEAD_WIDTH)
    value_tensor_three = values.reshape(TOKEN_COUNT, KEY_VALUE_HEADS, HEAD_WIDTH)
    weights_mask = label_mask.astype(jnp.float32)
    classes = jnp.arange(CLASSES, dtype=jnp.int32)

    def one_layer(carry, layer_in):
        key_gradient_sum, value_gradient_sum = carry
        query_layer, head_layer = layer_in
        loss_sum = jnp.zeros((), jnp.float32)
        head_grad = jnp.zeros((QUERY_HEADS * HEAD_WIDTH, CLASSES), jnp.float32)
        dq_rows = []
        for block in range(N_CTX):
            lower_limit = block * LOCAL_TOKENS
            upper_limit = lower_limit + LOCAL_TOKENS
            query_tensor_four = query_layer[lower_limit:upper_limit].reshape(LOCAL_TOKENS, KEY_VALUE_HEADS, head_group, HEAD_WIDTH)
            k_part = key_tensor_three[:upper_limit]
            v_part = value_tensor_three[:upper_limit].astype(jnp.float32)
            s = masked_scores(query_tensor_four, k_part, segments[lower_limit:upper_limit], segments[:upper_limit], lower_limit, 0)
            top = jnp.max(s, axis=-1)
            lse = top + jnp.log(jnp.sum(jnp.exp(s - top[..., None]), axis=-1))
            prob = jnp.exp(s - lse[..., None])
            attended = jnp.einsum("tgrn,ngd->tgrd", prob, v_part, precision=HIGH)
            flat_rows = attended.reshape(LOCAL_TOKENS, QUERY_HEADS * HEAD_WIDTH)
            logits = jnp.dot(flat_rows, head_layer, precision=HIGH)
            mx = jnp.max(logits, axis=-1)
            log_total = mx + jnp.log(jnp.sum(jnp.exp(logits - mx[:, None]), axis=-1))
            onehot = (labels[lower_limit:upper_limit, None] == classes[None, :]).astype(jnp.float32)
            mask = weights_mask[lower_limit:upper_limit]
            loss_sum = loss_sum + jnp.sum(mask * (log_total - jnp.sum(onehot * logits, axis=-1)))
            d_logits = mask[:, None] * (jnp.exp(logits - log_total[:, None]) - onehot)
            head_grad = head_grad + jnp.dot(flat_rows.T, d_logits, precision=HIGH)
            attention_gradient = jnp.dot(d_logits, head_layer.T, precision=HIGH)
            delta_rows = jnp.sum((attention_gradient * flat_rows).reshape(LOCAL_TOKENS, KEY_VALUE_HEADS, head_group, HEAD_WIDTH), axis=-1)
            attention_gradient_half = attention_gradient.astype(jnp.bfloat16).reshape(LOCAL_TOKENS, KEY_VALUE_HEADS, head_group, HEAD_WIDTH).astype(jnp.float32)
            prob16 = prob.astype(jnp.bfloat16).astype(jnp.float32)
            dv_t = jnp.einsum("tgrn,tgrd->ngd", prob16, attention_gradient_half, precision=HIGH)
            dp = jnp.einsum("tgrd,ngd->tgrn", attention_gradient_half, v_part, precision=HIGH)
            ds16 = (prob * (dp - delta_rows[..., None]) * (HEAD_WIDTH ** -0.5)).astype(jnp.bfloat16).astype(jnp.float32)
            dq_t = jnp.einsum("tgrn,ngd->tgrd", ds16, k_part.astype(jnp.float32), precision=HIGH)
            dk_t = jnp.einsum("tgrn,tgrd->ngd", ds16, query_tensor_four.astype(jnp.float32), precision=HIGH)
            pad = ((0, TOKEN_COUNT - upper_limit), (0, 0), (0, 0))
            key_gradient_sum = key_gradient_sum + jnp.pad(dk_t, pad)
            value_gradient_sum = value_gradient_sum + jnp.pad(dv_t, pad)
            dq_rows.append(dq_t.reshape(LOCAL_TOKENS, QUERY_HEADS * HEAD_WIDTH))
        return (key_gradient_sum, value_gradient_sum), (loss_sum / TOKEN_COUNT, jnp.concatenate(dq_rows, axis=0), head_grad)

    start_offset = (jnp.zeros((TOKEN_COUNT, KEY_VALUE_HEADS, HEAD_WIDTH), jnp.float32), jnp.zeros((TOKEN_COUNT, KEY_VALUE_HEADS, HEAD_WIDTH), jnp.float32))
    (key_gradient_sum, value_gradient_sum), (loss, query_gradient, head_gradient_rows) = lax.scan(one_layer, start_offset, (queries, head))
    return loss, query_gradient, key_gradient_sum.reshape(TOKEN_COUNT, KEY_VALUE_HEADS * HEAD_WIDTH), value_gradient_sum.reshape(TOKEN_COUNT, KEY_VALUE_HEADS * HEAD_WIDTH), head_gradient_rows
```

```python
import functools

import jax
import jax.numpy as jnp
from jax import lax
from jax.experimental import pallas as pl
from jax.experimental.pallas import tpu as pltpu
from jax.sharding import PartitionSpec as P

QUERY_HEADS = 12
KEY_VALUE_HEADS = 4
HEAD_WIDTH = 128

GROUP = QUERY_HEADS // KEY_VALUE_HEADS
LOG2_E = 1.4426950408889634
NEGATIVE_FILL = -1e30
HIGH = lax.Precision.HIGHEST
MESH = pl.DeviceIdType.MESH
STAT_ROWS = 8


def dot(a, b, a_dim, b_dim, precision=None):
    return lax.dot_general(
        a, b, (((a_dim,), (b_dim,)), ((), ())), precision=precision,
        preferred_element_type=jnp.float32,
    )


def kernel(
    n_layer, n_ctx, q_ref, k_ref, v_ref, head_ref, seg_ref, mask_ref, label_ref,
    loss_ref, dq_ref, gk_ref, gv_ref, hg_ref,
    kv, score, hb, peak, total, att, datt, delta, dqt, grad, stats,
    send_ctx, recv_ctx, send_x, recv_x, send_z, recv_z,
    gz_s, gz_r, gx_s, gx_r, gc_s, gc_r, st_s, st_r, rc_s, rc_r, rx_s, rx_r, rz_s, rz_r,
):
    W = HEAD_WIDTH
    local = q_ref.shape[0]
    rows = k_ref.shape[0]
    classes = head_ref.shape[0]
    n_high = n_layer // 2
    layer, ctx = lax.axis_index("layer"), lax.axis_index("ctx")
    high, low = layer // 2, layer % 2
    twin = high * 2 + (1 - low)
    tail = (3 * n_ctx) // 4
    in_tail = (ctx >= tail).astype(jnp.int32)
    first = in_tail * tail
    end = tail + in_tail * (n_ctx - tail)
    count = ctx - first + 1

    def remote(src, dst, s, r, to_layer, to_ctx):
        return pltpu.make_async_remote_copy(
            src_ref=src, dst_ref=dst, send_sem=s, recv_sem=r,
            device_id=(to_layer, to_ctx), device_id_type=MESH,
        )

    kv[ctx, layer, 0] = k_ref[...]
    kv[ctx, layer, 1] = v_ref[...]

    barrier = pltpu.get_barrier_semaphore()
    for d in range(1, n_high):
        pl.semaphore_signal(
            barrier, inc=1, device_id=(lax.rem(high + d, n_high) * 2 + low, ctx),
            device_id_type=MESH)
    pl.semaphore_signal(barrier, inc=1, device_id=(twin, ctx), device_id_type=MESH)
    for d in range(1, n_ctx):
        pl.semaphore_signal(
            barrier, inc=1, device_id=(layer, lax.rem(ctx + d, n_ctx)), device_id_type=MESH)
    pl.semaphore_wait(barrier, n_high + n_ctx - 1)

    def to_later(piece):
        def one(to, carry):
            remote(kv.at[ctx, piece], kv.at[ctx, piece], gc_s.at[to], gc_r.at[ctx],
                   layer, to).start()
            return carry
        lax.fori_loop(ctx + 1, end, one, 0)

    def line_copy(d):
        return remote(kv.at[ctx, layer], kv.at[ctx, layer], gz_s.at[d], gz_r.at[d],
                      lax.rem(high + d, n_high) * 2 + low, ctx)

    def twin_copy(d, side):
        piece = lax.rem(high + n_high - d, n_high) * 2 + side
        return remote(kv.at[ctx, piece], kv.at[ctx, piece], gx_s.at[d], gx_r.at[d], twin, ctx)

    for d in range(1, n_high):
        line_copy(d).start()
    twin_copy(0, low).start()
    to_later(layer)

    for k in range(classes):
        for h in range(QUERY_HEADS):
            row = head_ref[k : k + 1, h * W : (h + 1) * W]
            hb[k, h] = jnp.transpose(jnp.broadcast_to(row, (local, W)))

    for d in range(1, n_high):
        piece = lax.rem(high + n_high - d, n_high) * 2 + low
        remote(kv.at[ctx, piece], kv.at[ctx, piece], gz_s.at[d], gz_r.at[d],
               layer, ctx).wait_recv()
        twin_copy(d, low).start()
        to_later(piece)
    for d in range(n_high):
        twin_copy(d, 1 - low).wait_recv()
        to_later(lax.rem(high + n_high - d, n_high) * 2 + (1 - low))

    def block_of(j, which, g):
        part = kv[j, :, which, :, g * W : (g + 1) * W]
        if rows % 16:
            return part.astype(jnp.float32).reshape(n_layer * rows, W).astype(jnp.bfloat16)
        return part.reshape(n_layer * rows, W)

    def query_of(g):
        return jnp.concatenate(
            [q_ref[:, (g * GROUP + r) * W : (g * GROUP + r + 1) * W] for r in range(GROUP)], axis=0)

    peak[...] = jnp.full_like(peak, NEGATIVE_FILL)
    total[...] = jnp.zeros_like(total)
    att[...] = jnp.zeros_like(att)
    dqt[...] = jnp.zeros_like(dqt)

    seg_q = seg_ref[pl.ds(ctx, 1), :]

    def score_block(i, carry):
        j = ctx - i

        @pl.when(i > 0)
        def _():
            remote(kv.at[j], kv.at[j], gc_s.at[j], gc_r.at[j], layer, ctx).wait_recv()

        seg_k = jnp.transpose(
            jnp.broadcast_to(seg_ref[pl.ds(j, 1), :], (local, local)).astype(jnp.float32))
        same = seg_k == jnp.broadcast_to(seg_q, (local, local)).astype(jnp.float32)
        k_pos = j * local + lax.broadcasted_iota(jnp.int32, (local, local), 0)
        q_pos = ctx * local + lax.broadcasted_iota(jnp.int32, (local, local), 1)
        fill = jnp.where(same & (k_pos <= q_pos), 0.0, NEGATIVE_FILL)
        fill = jnp.concatenate([fill] * GROUP, axis=1)
        for g in range(KEY_VALUE_HEADS):
            s = dot(block_of(j, 0, g), query_of(g), 1, 1) * (LOG2_E * W ** -0.5)
            s = jnp.where(fill < 0.0, NEGATIVE_FILL, s)
            score[j, g] = s
            peak[g] = jnp.maximum(peak[g], jnp.max(s, axis=0, keepdims=True))
        return carry

    lax.fori_loop(0, count, score_block, 0)

    def weigh_block(i, carry):
        j = ctx - i
        for g in range(KEY_VALUE_HEADS):
            p = jnp.exp2(score[j, g] - peak[g])
            score[j, g] = p
            total[g] += jnp.sum(p, axis=0, keepdims=True)
            att[g] += dot(block_of(j, 1, g), p.astype(jnp.bfloat16), 0, 0)
        return carry

    lax.fori_loop(0, count, weigh_block, 0)

    logits = [jnp.zeros((1, local), jnp.float32) for _ in range(classes)]
    parts = []
    for g in range(KEY_VALUE_HEADS):
        inverse = 1.0 / total[g]
        total[g] = inverse
        att[g] = att[g] * inverse
        for r in range(GROUP):
            a = att[g, :, r * W : (r + 1) * W]
            part = [jnp.sum(hb[k, g * GROUP + r] * a, axis=0, keepdims=True)
                    for k in range(classes)]
            parts.append(part)
            logits = [x + y for x, y in zip(logits, part)]
    biggest = functools.reduce(jnp.maximum, logits)
    log_total = biggest + jnp.log(sum(jnp.exp(x - biggest) for x in logits))
    mask = mask_ref[...].astype(jnp.float32)
    hot = [(label_ref[...] == k).astype(jnp.float32) for k in range(classes)]
    loss_rows = mask * (log_total - sum(o * x for o, x in zip(hot, logits)))
    d_logits = [mask * (jnp.exp(x - log_total) - o) for o, x in zip(hot, logits)]

    stacked = jnp.concatenate(
        d_logits + [jnp.zeros((STAT_ROWS - classes, local), jnp.float32)], axis=0)
    for h in range(QUERY_HEADS):
        g, r = h // GROUP, h % GROUP
        cols = slice(r * W, (r + 1) * W)
        stats[ctx, :, h * W : (h + 1) * W] = dot(stacked, att[g, :, cols], 1, 1, HIGH)
        da = sum(hb[k, h] * d_logits[k] for k in range(classes))
        datt[g, :, cols] = da.astype(jnp.bfloat16)
        delta[g, :, cols] = sum(parts[h][k] * d_logits[k] for k in range(classes))
    stats[ctx, classes : classes + 1, 0:local] = loss_rows

    for d in range(1, n_ctx):
        remote(stats.at[ctx], stats.at[ctx], st_s.at[d], st_r.at[d],
               layer, lax.rem(ctx + d, n_ctx)).start()

    def back_block(i, carry):
        j = first + i
        for g in range(KEY_VALUE_HEADS):
            k_block, v_block = block_of(j, 0, g), block_of(j, 1, g)
            da = datt[g]
            dp = dot(v_block, da, 1, 0)
            prob = score[j, g] * total[g]
            ds = (prob * ((dp - delta[g]) * W ** -0.5)).astype(jnp.bfloat16)
            dqt[g] += dot(k_block, ds, 0, 0)
            cols = slice(g * W, (g + 1) * W)
            grad[:, 0, :, cols] = dot(ds, query_of(g), 1, 0).reshape(n_layer, rows, W)
            grad[:, 1, :, cols] = dot(prob.astype(jnp.bfloat16), da, 1, 1).reshape(
                n_layer, rows, W)

        @pl.when(j < ctx)
        def _():
            send_ctx[j] = grad[...].astype(jnp.bfloat16)
            remote(send_ctx.at[j], recv_ctx.at[ctx], rc_s.at[j], rc_r.at[ctx], layer, j).start()

        return carry

    lax.fori_loop(0, count, back_block, 0)

    def gather_later(i, carry):
        remote(send_ctx.at[i], recv_ctx.at[i], rc_s.at[i], rc_r.at[i], layer, ctx).wait_recv()
        grad[...] = grad[...] + recv_ctx[i].astype(jnp.float32)
        return carry

    lax.fori_loop(ctx + 1, end, gather_later, 0)

    for z in range(n_high):
        send_x[z] = grad[z * 2 + (1 - low)].astype(jnp.bfloat16)
    x_copy = remote(send_x, recv_x, rx_s, rx_r, twin, ctx)
    x_copy.start()

    for h in range(QUERY_HEADS):
        g, r = h // GROUP, h % GROUP
        dq_ref[:, h * W : (h + 1) * W] = jnp.transpose(dqt[g, :, r * W : (r + 1) * W])

    x_copy.wait_recv()
    z_copies = []
    for d in range(1, n_high):
        to = lax.rem(high + d, n_high)
        send_z[d] = (grad[to * 2 + low] + recv_x[to].astype(jnp.float32)).astype(jnp.bfloat16)
        copy = remote(send_z.at[d], recv_z.at[d], rz_s.at[d], rz_r.at[d], to * 2 + low, ctx)
        copy.start()
        z_copies.append(copy)
    mine = grad[high * 2 + low] + recv_x[high].astype(jnp.float32)

    for d in range(1, n_ctx):
        origin = lax.rem(ctx + n_ctx - d, n_ctx)
        remote(stats.at[origin], stats.at[origin], st_s.at[d], st_r.at[d],
               layer, ctx).wait_recv()
    whole = stats[0]
    for j in range(1, n_ctx):
        whole = whole + stats[j]
    hg_ref[...] = whole[0:classes]
    loss_ref[0] = jnp.sum(whole[classes : classes + 1, 0:local]) * (1.0 / (local * n_ctx))

    for d in range(1, n_high):
        z_copies[d - 1].wait_recv()
        mine = mine + recv_z[d].astype(jnp.float32)
    gk_ref[...] = mine[0]
    gv_ref[...] = mine[1]

    for d in range(1, n_high):
        line_copy(d).wait_send()
        z_copies[d - 1].wait_send()
    for d in range(n_high):
        twin_copy(d, low).wait_send()
    for d in range(1, n_ctx):
        remote(stats.at[ctx], stats.at[ctx], st_s.at[d], st_r.at[d],
               layer, lax.rem(ctx + d, n_ctx)).wait_send()
    x_copy.wait_send()

    def sent_later(to, carry):
        remote(kv.at[ctx], kv.at[ctx], gc_s.at[to], gc_r.at[ctx], layer, to).wait_send()
        return carry

    lax.fori_loop(ctx + 1, end, sent_later, 0)

    def sent_back(j, carry):
        remote(send_ctx.at[j], recv_ctx.at[ctx], rc_s.at[j], rc_r.at[ctx], layer, j).wait_send()
        return carry

    lax.fori_loop(first, ctx, sent_back, 0)


def per_device(queries, keys, values, head, segments, label_mask, labels):
    n_layer, n_ctx = lax.axis_size("layer"), lax.axis_size("ctx")
    local, width = queries.shape[1:]
    rows, kv_width = keys.shape
    classes = head.shape[2]
    n_high = n_layer // 2
    G, W, T = KEY_VALUE_HEADS, HEAD_WIDTH, GROUP * local
    vmem = pl.BlockSpec(memory_space=pltpu.VMEM)
    bf, f32 = jnp.bfloat16, jnp.float32
    dma = pltpu.SemaphoreType.DMA
    loss, dq, gk, gv, hg = pl.pallas_call(
        functools.partial(kernel, n_layer, n_ctx),
        out_shape=(
            jax.ShapeDtypeStruct((1,), f32),
            jax.ShapeDtypeStruct((local, width), f32),
            jax.ShapeDtypeStruct((rows, kv_width), f32),
            jax.ShapeDtypeStruct((rows, kv_width), f32),
            jax.ShapeDtypeStruct((classes, width), f32),
        ),
        in_specs=[vmem] * 7,
        out_specs=(pl.BlockSpec(memory_space=pltpu.SMEM), vmem, vmem, vmem, vmem),
        scratch_shapes=[
            pltpu.VMEM((n_ctx, n_layer, 2, rows, kv_width), bf),
            pltpu.VMEM((n_ctx, G, local, T), f32),
            pltpu.VMEM((classes, QUERY_HEADS, W, local), f32),
            pltpu.VMEM((G, 1, T), f32),
            pltpu.VMEM((G, 1, T), f32),
            pltpu.VMEM((G, W, T), f32),
            pltpu.VMEM((G, W, T), bf),
            pltpu.VMEM((G, 1, T), f32),
            pltpu.VMEM((G, W, T), f32),
            pltpu.VMEM((n_layer, 2, rows, kv_width), f32),
            pltpu.VMEM((n_ctx, STAT_ROWS, width), f32),
            pltpu.VMEM((n_ctx, n_layer, 2, rows, kv_width), bf),
            pltpu.VMEM((n_ctx, n_layer, 2, rows, kv_width), bf),
            pltpu.VMEM((n_high, 2, rows, kv_width), bf),
            pltpu.VMEM((n_high, 2, rows, kv_width), bf),
            pltpu.VMEM((n_high, 2, rows, kv_width), bf),
            pltpu.VMEM((n_high, 2, rows, kv_width), bf),
            dma((n_high,)), dma((n_high,)), dma((n_high,)), dma((n_high,)),
            dma((n_ctx,)), dma((n_ctx,)), dma((n_ctx,)), dma((n_ctx,)),
            dma((n_ctx,)), dma((n_ctx,)), dma, dma,
            dma((n_high,)), dma((n_high,)),
        ],
        compiler_params=pltpu.CompilerParams(
            collective_id=0, has_side_effects=True, vmem_limit_bytes=48 * 1024 * 1024),
    )(
        queries[0], keys, values, jnp.swapaxes(head[0], 0, 1),
        segments.reshape(n_ctx, local), label_mask[None], labels[None],
    )
    return loss, dq[None], gk, gv, jnp.swapaxes(hg, 0, 1)[None]


def solution(mesh):
    return jax.shard_map(
        per_device,
        mesh=mesh,
        in_specs=(
            P("layer", "ctx", None),
            P(("ctx", "layer"), None),
            P(("ctx", "layer"), None),
            P("layer", None, None),
            P(),
            P("ctx"),
            P("ctx"),
        ),
        out_specs=(
            P("layer"),
            P("layer", "ctx", None),
            P(("ctx", "layer"), None),
            P(("ctx", "layer"), None),
            P("layer", None, None),
        ),
        check_vma=False,
    )
```

```python
import functools

import jax
import jax.numpy as jnp
from jax import lax
from jax.experimental import pallas as pl
from jax.experimental.pallas import tpu as pltpu
from jax.sharding import PartitionSpec as P

QUERY_HEADS = 12
KEY_VALUE_HEADS = 4
HEAD_WIDTH = 128

GROUP = QUERY_HEADS // KEY_VALUE_HEADS
LOG2_E = 1.4426950408889634
NEGATIVE_FILL = -1e30
HIGH = lax.Precision.HIGHEST
MESH = pl.DeviceIdType.MESH
STAT_ROWS = 8


def dot(a, b, a_dim, b_dim, precision=None):
    return lax.dot_general(
        a, b, (((a_dim,), (b_dim,)), ((), ())), precision=precision,
        preferred_element_type=jnp.float32,
    )


def kernel(
    n_layer, n_ctx, q_in, k_in, v_in, head_in, seg_in, mask_in, label_in,
    loss_ref, dq_ref, gk_ref, gv_ref, hg_ref,
    q_ref, head_ref, seg_ref, mask_ref, label_ref, in_sem,
    kv, score, hb, peak, tops, total, att, datt, delta, dqt, grad, mine, rows_d, stats,
    send_ctx, recv_ctx, send_x, recv_x, send_z, recv_z,
    gz_s, gz_r, gx_s, gx_r, gc_s, gc_r, st_s, st_r, rc_s, rc_r, rx_s, rx_r, rz_s, rz_r,
):
    W = HEAD_WIDTH
    local = q_ref.shape[0]
    rows = k_in.shape[0]
    classes = head_ref.shape[0]
    n_high = n_layer // 2
    layer, ctx = lax.axis_index("layer"), lax.axis_index("ctx")
    high, low = layer // 2, layer % 2
    twin = high * 2 + (1 - low)
    tail = (3 * n_ctx) // 4
    in_tail = (ctx >= tail).astype(jnp.int32)
    first = in_tail * tail
    end = tail + in_tail * (n_ctx - tail)
    count = ctx - first + 1

    def remote(src, dst, s, r, to_layer, to_ctx):
        return pltpu.make_async_remote_copy(
            src_ref=src, dst_ref=dst, send_sem=s, recv_sem=r,
            device_id=(to_layer, to_ctx), device_id_type=MESH,
        )

    k_load, v_load, head_load, q_load, *small_loads = [
        pltpu.make_async_copy(src, dst, in_sem.at[i])
        for i, (src, dst) in enumerate([
            (k_in, kv.at[ctx, layer, 0]), (v_in, kv.at[ctx, layer, 1]), (head_in, head_ref),
            (q_in, q_ref), (seg_in, seg_ref), (mask_in, mask_ref), (label_in, label_ref)])
    ]
    for load in (k_load, v_load, head_load, q_load, *small_loads):
        load.start()

    barrier = pltpu.get_barrier_semaphore()
    for d in range(1, n_high):
        pl.semaphore_signal(
            barrier, inc=1, device_id=(lax.rem(high + d, n_high) * 2 + low, ctx),
            device_id_type=MESH)
    pl.semaphore_signal(barrier, inc=1, device_id=(twin, ctx), device_id_type=MESH)
    for d in range(1, n_ctx):
        pl.semaphore_signal(
            barrier, inc=1, device_id=(layer, lax.rem(ctx + d, n_ctx)), device_id_type=MESH)
    head_load.wait()
    for k in range(classes):
        for h in range(QUERY_HEADS):
            row = head_ref[k : k + 1, h * W : (h + 1) * W]
            hb[k, h] = jnp.transpose(jnp.broadcast_to(row, (local, W)))

    k_load.wait()
    v_load.wait()
    pl.semaphore_wait(barrier, n_high + n_ctx - 1)

    def to_later(piece):
        def one(to, carry):
            remote(kv.at[ctx, piece], kv.at[ctx, piece], gc_s.at[to], gc_r.at[ctx],
                   layer, to).start()
            return carry
        lax.fori_loop(ctx + 1, end, one, 0)

    def line_copy(d):
        return remote(kv.at[ctx, layer], kv.at[ctx, layer], gz_s.at[d], gz_r.at[d],
                      lax.rem(high + d, n_high) * 2 + low, ctx)

    def twin_copy(d, side):
        piece = lax.rem(high + n_high - d, n_high) * 2 + side
        return remote(kv.at[ctx, piece], kv.at[ctx, piece], gx_s.at[d], gx_r.at[d], twin, ctx)

    for d in range(1, n_high):
        line_copy(d).start()
    twin_copy(0, low).start()
    to_later(layer)

    for d in range(1, n_high):
        piece = lax.rem(high + n_high - d, n_high) * 2 + low
        remote(kv.at[ctx, piece], kv.at[ctx, piece], gz_s.at[d], gz_r.at[d],
               layer, ctx).wait_recv()
        twin_copy(d, low).start()
        to_later(piece)
    for d in range(n_high):
        twin_copy(d, 1 - low).wait_recv()
        to_later(lax.rem(high + n_high - d, n_high) * 2 + (1 - low))

    def block_of(j, which, g):
        part = kv[j, :, which, :, g * W : (g + 1) * W]
        if rows % 16:
            return part.astype(jnp.float32).reshape(n_layer * rows, W).astype(jnp.bfloat16)
        return part.reshape(n_layer * rows, W)

    def query_of(g):
        return jnp.concatenate(
            [q_ref[:, (g * GROUP + r) * W : (g * GROUP + r + 1) * W] for r in range(GROUP)], axis=0)

    peak[...] = jnp.full_like(peak, NEGATIVE_FILL)
    total[...] = jnp.zeros_like(total)
    att[...] = jnp.zeros_like(att)
    dqt[...] = jnp.zeros_like(dqt)

    for load in (q_load, *small_loads):
        load.wait()
    seg_q = seg_ref[pl.ds(ctx, 1), :]

    def score_block(i, carry):
        j = ctx - i

        @pl.when(i > 0)
        def _():
            remote(kv.at[j], kv.at[j], gc_s.at[j], gc_r.at[j], layer, ctx).wait_recv()

        seg_k = jnp.transpose(
            jnp.broadcast_to(seg_ref[pl.ds(j, 1), :], (local, local)).astype(jnp.float32))
        same = seg_k == jnp.broadcast_to(seg_q, (local, local)).astype(jnp.float32)
        k_pos = j * local + lax.broadcasted_iota(jnp.int32, (local, local), 0)
        q_pos = ctx * local + lax.broadcasted_iota(jnp.int32, (local, local), 1)
        fill = jnp.where(same & (k_pos <= q_pos), 0.0, NEGATIVE_FILL)
        fill = jnp.concatenate([fill] * GROUP, axis=1)
        for g in range(KEY_VALUE_HEADS):
            s = dot(block_of(j, 0, g), query_of(g), 1, 1) * (LOG2_E * W ** -0.5)
            s = jnp.where(fill < 0.0, NEGATIVE_FILL, s)
            top = jnp.maximum(peak[g], jnp.max(s, axis=0, keepdims=True))
            fade = jnp.exp2(peak[g] - top)
            p = jnp.exp2(s - top)
            score[j, g] = p
            tops[j, g] = top
            peak[g] = top
            total[g] = total[g] * fade + jnp.sum(p, axis=0, keepdims=True)
            att[g] = att[g] * fade + dot(block_of(j, 1, g), p.astype(jnp.bfloat16), 0, 0)
        return carry

    lax.fori_loop(0, count, score_block, 0)

    logits = [jnp.zeros((1, local), jnp.float32) for _ in range(classes)]
    parts = []
    for g in range(KEY_VALUE_HEADS):
        inverse = 1.0 / total[g]
        total[g] = inverse
        att[g] = att[g] * inverse
        for r in range(GROUP):
            a = att[g, :, r * W : (r + 1) * W]
            part = [jnp.sum(hb[k, g * GROUP + r] * a, axis=0, keepdims=True)
                    for k in range(classes)]
            parts.append(part)
            logits = [x + y for x, y in zip(logits, part)]
    biggest = functools.reduce(jnp.maximum, logits)
    log_total = biggest + jnp.log(sum(jnp.exp(x - biggest) for x in logits))
    mask = mask_ref[...].astype(jnp.float32)
    hot = [(label_ref[...] == k).astype(jnp.float32) for k in range(classes)]
    loss_rows = mask * (log_total - sum(o * x for o, x in zip(hot, logits)))
    d_logits = [mask * (jnp.exp(x - log_total) - o) for o, x in zip(hot, logits)]

    for h in range(QUERY_HEADS):
        g, r = h // GROUP, h % GROUP
        cols = slice(r * W, (r + 1) * W)
        da = sum(hb[k, h] * d_logits[k] for k in range(classes))
        datt[g, :, cols] = da.astype(jnp.bfloat16)
        delta[g, :, cols] = sum(parts[h][k] * d_logits[k] for k in range(classes))
    for k in range(classes):
        rows_d[k : k + 1, :] = d_logits[k]
    rows_d[classes : classes + 1, :] = loss_rows

    def back_block(i, carry):
        j = first + i
        for g in range(KEY_VALUE_HEADS):
            k_block, v_block = block_of(j, 0, g), block_of(j, 1, g)
            da = datt[g]
            dp = dot(v_block, da, 1, 0)
            prob = score[j, g] * (total[g] * jnp.exp2(tops[j, g] - peak[g]))
            ds = (prob * ((dp - delta[g]) * W ** -0.5)).astype(jnp.bfloat16)
            dqt[g] += dot(k_block, ds, 0, 0)
            cols = slice(g * W, (g + 1) * W)
            grad[:, 0, :, cols] = dot(ds, query_of(g), 1, 0).reshape(n_layer, rows, W)
            grad[:, 1, :, cols] = dot(prob.astype(jnp.bfloat16), da, 1, 1).reshape(
                n_layer, rows, W)

        @pl.when(j < ctx)
        def _():
            send_ctx[j] = grad[...].astype(jnp.bfloat16)
            for d in range(n_high):
                part = pl.ds(lax.rem(high + 1 + d, n_high) * 2, 2)
                remote(send_ctx.at[j, part], recv_ctx.at[ctx, part], rc_s.at[j],
                       rc_r.at[ctx, d], layer, j).start()

        return carry

    lax.fori_loop(0, count, back_block, 0)

    def side_work():
        stacked = jnp.concatenate(
            [rows_d[0:classes, :], jnp.zeros((STAT_ROWS - classes, local), jnp.float32)], axis=0)
        for h in range(QUERY_HEADS):
            g, r = h // GROUP, h % GROUP
            stats[ctx, :, h * W : (h + 1) * W] = dot(
                stacked, att[g, :, r * W : (r + 1) * W], 1, 1, HIGH)
        stats[ctx, classes : classes + 1, 0:local] = rows_d[classes : classes + 1, :]
        for d in range(1, n_ctx):
            remote(stats.at[ctx], stats.at[ctx], st_s.at[d], st_r.at[d],
                   layer, lax.rem(ctx + d, n_ctx)).start()
        for h in range(QUERY_HEADS):
            g, r = h // GROUP, h % GROUP
            dq_ref[:, h * W : (h + 1) * W] = jnp.transpose(dqt[g, :, r * W : (r + 1) * W])

    def place(d):
        return lax.rem(high + 1 + d, n_high)

    def x_copy(d):
        return remote(send_x.at[d], recv_x.at[d], rx_s.at[d], rx_r.at[d], twin, ctx)

    def z_copy(d):
        return remote(send_z.at[d], recv_z.at[d], rz_s.at[d], rz_r.at[d],
                      place(d) * 2 + low, ctx)

    def x_stage(d):
        part = pl.ds(place(d) * 2, 2)

        def one(i, carry):
            remote(send_ctx.at[i, part], recv_ctx.at[i, part], rc_s.at[i], rc_r.at[i, d],
                   layer, ctx).wait_recv()
            grad[part] = grad[part] + recv_ctx[i, part].astype(jnp.float32)
            return carry

        lax.fori_loop(ctx + 1, end, one, 0)
        send_x[d] = grad[place(d) * 2 + (1 - low)].astype(jnp.bfloat16)
        x_copy(d).start()

    def z_stage(d):
        x_copy(d).wait_recv()
        value = grad[place(d) * 2 + low] + recv_x[d].astype(jnp.float32)
        if d < n_high - 1:
            send_z[d] = value.astype(jnp.bfloat16)
            z_copy(d).start()
        else:
            mine[...] = value

    @pl.when(ctx < end - 1)
    def _():
        side_work()
        for d in range(n_high):
            x_stage(d)
            if d:
                z_stage(d - 1)
        z_stage(n_high - 1)

    @pl.when(ctx == end - 1)
    def _():
        for d in range(n_high):
            x_stage(d)
        side_work()
        for d in range(n_high):
            z_stage(d)

    for d in range(1, n_ctx):
        origin = lax.rem(ctx + n_ctx - d, n_ctx)
        remote(stats.at[origin], stats.at[origin], st_s.at[d], st_r.at[d],
               layer, ctx).wait_recv()
    whole = stats[0]
    for j in range(1, n_ctx):
        whole = whole + stats[j]
    hg_ref[...] = whole[0:classes]
    loss_ref[0] = jnp.sum(whole[classes : classes + 1, 0:local]) * (1.0 / (local * n_ctx))

    result = mine[...]
    for d in range(n_high - 1):
        z_copy(d).wait_recv()
        result = result + recv_z[d].astype(jnp.float32)
    gk_ref[...] = result[0]
    gv_ref[...] = result[1]

    for d in range(1, n_high):
        line_copy(d).wait_send()
    for d in range(n_high - 1):
        z_copy(d).wait_send()
    for d in range(n_high):
        twin_copy(d, low).wait_send()
        x_copy(d).wait_send()
    for d in range(1, n_ctx):
        remote(stats.at[ctx], stats.at[ctx], st_s.at[d], st_r.at[d],
               layer, lax.rem(ctx + d, n_ctx)).wait_send()

    def sent_later(to, carry):
        remote(kv.at[ctx], kv.at[ctx], gc_s.at[to], gc_r.at[ctx], layer, to).wait_send()
        return carry

    lax.fori_loop(ctx + 1, end, sent_later, 0)

    def sent_back(j, carry):
        remote(send_ctx.at[j], recv_ctx.at[ctx], rc_s.at[j], rc_r.at[ctx, 0], layer, j).wait_send()
        return carry

    lax.fori_loop(first, ctx, sent_back, 0)


def per_device(queries, keys, values, head, segments, label_mask, labels):
    n_layer, n_ctx = lax.axis_size("layer"), lax.axis_size("ctx")
    local, width = queries.shape[1:]
    rows, kv_width = keys.shape
    classes = head.shape[2]
    n_high = n_layer // 2
    G, W, T = KEY_VALUE_HEADS, HEAD_WIDTH, GROUP * local
    vmem = pl.BlockSpec(memory_space=pltpu.VMEM)
    bf, f32 = jnp.bfloat16, jnp.float32
    dma = pltpu.SemaphoreType.DMA
    loss, dq, gk, gv, hg = pl.pallas_call(
        functools.partial(kernel, n_layer, n_ctx),
        out_shape=(
            jax.ShapeDtypeStruct((1,), f32),
            jax.ShapeDtypeStruct((local, width), f32),
            jax.ShapeDtypeStruct((rows, kv_width), f32),
            jax.ShapeDtypeStruct((rows, kv_width), f32),
            jax.ShapeDtypeStruct((classes, width), f32),
        ),
        in_specs=[pl.BlockSpec(memory_space=pltpu.HBM)] * 7,
        out_specs=(pl.BlockSpec(memory_space=pltpu.SMEM), vmem, vmem, vmem, vmem),
        scratch_shapes=[
            pltpu.VMEM((local, width), bf),
            pltpu.VMEM((classes, width), f32),
            pltpu.VMEM((n_ctx, local), jnp.int32),
            pltpu.VMEM((1, local), jnp.int32),
            pltpu.VMEM((1, local), jnp.int32),
            dma((7,)),
            pltpu.VMEM((n_ctx, n_layer, 2, rows, kv_width), bf),
            pltpu.VMEM((n_ctx, G, local, T), f32),
            pltpu.VMEM((classes, QUERY_HEADS, W, local), f32),
            pltpu.VMEM((G, 1, T), f32),
            pltpu.VMEM((n_ctx, G, 1, T), f32),
            pltpu.VMEM((G, 1, T), f32),
            pltpu.VMEM((G, W, T), f32),
            pltpu.VMEM((G, W, T), bf),
            pltpu.VMEM((G, 1, T), f32),
            pltpu.VMEM((G, W, T), f32),
            pltpu.VMEM((n_layer, 2, rows, kv_width), f32),
            pltpu.VMEM((2, rows, kv_width), f32),
            pltpu.VMEM((STAT_ROWS, local), f32),
            pltpu.VMEM((n_ctx, STAT_ROWS, width), f32),
            pltpu.VMEM((n_ctx, n_layer, 2, rows, kv_width), bf),
            pltpu.VMEM((n_ctx, n_layer, 2, rows, kv_width), bf),
            pltpu.VMEM((n_high, 2, rows, kv_width), bf),
            pltpu.VMEM((n_high, 2, rows, kv_width), bf),
            pltpu.VMEM((n_high, 2, rows, kv_width), bf),
            pltpu.VMEM((n_high, 2, rows, kv_width), bf),
            dma((n_high,)), dma((n_high,)), dma((n_high,)), dma((n_high,)),
            dma((n_ctx,)), dma((n_ctx,)), dma((n_ctx,)), dma((n_ctx,)),
            dma((n_ctx,)), dma((n_ctx, n_high)), dma((n_high,)), dma((n_high,)),
            dma((n_high,)), dma((n_high,)),
        ],
        compiler_params=pltpu.CompilerParams(
            collective_id=0, has_side_effects=True, vmem_limit_bytes=64 * 1024 * 1024 - 128 * 1024),
    )(
        queries[0], keys, values, jnp.swapaxes(head[0], 0, 1),
        segments.reshape(n_ctx, local), label_mask[None], labels[None],
    )
    return loss, dq[None], gk, gv, jnp.swapaxes(hg, 0, 1)[None]


def solution(mesh):
    return jax.shard_map(
        per_device,
        mesh=mesh,
        in_specs=(
            P("layer", "ctx", None),
            P(("ctx", "layer"), None),
            P(("ctx", "layer"), None),
            P("layer", None, None),
            P(),
            P("ctx"),
            P("ctx"),
        ),
        out_specs=(
            P("layer"),
            P("layer", "ctx", None),
            P(("ctx", "layer"), None),
            P(("ctx", "layer"), None),
            P("layer", None, None),
        ),
        check_vma=False,
    )
```

```python
import functools

import jax
import jax.numpy as jnp
from jax import lax
from jax.experimental import pallas as pl
from jax.experimental.pallas import tpu as pltpu
from jax.sharding import PartitionSpec as P

QUERY_HEADS = 12
KEY_VALUE_HEADS = 4
HEAD_WIDTH = 128

GROUP = QUERY_HEADS // KEY_VALUE_HEADS
LOG2_E = 1.4426950408889634
NEGATIVE_FILL = -1e30
HIGH = lax.Precision.HIGHEST
MESH = pl.DeviceIdType.MESH
STAT_ROWS = 8


def dot(a, b, a_dim, b_dim, precision=None):
    return lax.dot_general(
        a, b, (((a_dim,), (b_dim,)), ((), ())), precision=precision,
        preferred_element_type=jnp.float32,
    )


def kernel(
    n_layer, n_ctx, q_in, k_in, v_in, head_in, seg_in, mask_in, label_in,
    loss_ref, dq_ref, gk_ref, gv_ref, hg_ref,
    q_ref, head_ref, seg_ref, mask_ref, label_ref, in_sem,
    kv, score, hb, peak, tops, total, att, datt, delta, dqt, grad, mine, rows_d, stats,
    send_ctx, recv_ctx, send_x, recv_x, send_z, recv_z,
    gz_s, gz_r, gx_s, gx_r, gc_s, gc_r, st_s, st_r, rc_s, rc_r, rx_s, rx_r, rz_s, rz_r,
):
    W = HEAD_WIDTH
    local = q_ref.shape[0]
    rows = k_in.shape[0]
    classes = head_ref.shape[0]
    n_high = n_layer // 2
    layer, ctx = lax.axis_index("layer"), lax.axis_index("ctx")
    high, low = layer // 2, layer % 2
    twin = high * 2 + (1 - low)
    tail = (3 * n_ctx) // 4
    in_tail = (ctx >= tail).astype(jnp.int32)
    first = in_tail * tail
    end = tail + in_tail * (n_ctx - tail)
    count = ctx - first + 1

    def remote(src, dst, s, r, to_layer, to_ctx):
        return pltpu.make_async_remote_copy(
            src_ref=src, dst_ref=dst, send_sem=s, recv_sem=r,
            device_id=(to_layer, to_ctx), device_id_type=MESH,
        )

    k_load, v_load, head_load, q_load, *small_loads = [
        pltpu.make_async_copy(src, dst, in_sem.at[i])
        for i, (src, dst) in enumerate([
            (k_in, kv.at[ctx, layer, 0]), (v_in, kv.at[ctx, layer, 1]), (head_in, head_ref),
            (q_in, q_ref), (seg_in, seg_ref), (mask_in, mask_ref), (label_in, label_ref)])
    ]
    for load in (k_load, v_load, head_load, q_load, *small_loads):
        load.start()

    barrier = pltpu.get_barrier_semaphore()
    for d in range(1, n_high):
        pl.semaphore_signal(
            barrier, inc=1, device_id=(lax.rem(high + d, n_high) * 2 + low, ctx),
            device_id_type=MESH)
    pl.semaphore_signal(barrier, inc=1, device_id=(twin, ctx), device_id_type=MESH)
    for d in range(1, n_ctx):
        pl.semaphore_signal(
            barrier, inc=1, device_id=(layer, lax.rem(ctx + d, n_ctx)), device_id_type=MESH)
    k_load.wait()
    v_load.wait()
    pl.semaphore_wait(barrier, n_high + n_ctx - 1)

    def to_later(piece):
        def one(to, carry):
            remote(kv.at[ctx, piece], kv.at[ctx, piece], gc_s.at[to], gc_r.at[ctx],
                   layer, to).start()
            return carry
        lax.fori_loop(ctx + 1, end, one, 0)

    def line_copy(d):
        return remote(kv.at[ctx, layer], kv.at[ctx, layer], gz_s.at[d], gz_r.at[d],
                      lax.rem(high + d, n_high) * 2 + low, ctx)

    def twin_copy(d, side):
        piece = lax.rem(high + n_high - d, n_high) * 2 + side
        return remote(kv.at[ctx, piece], kv.at[ctx, piece], gx_s.at[d], gx_r.at[d], twin, ctx)

    for d in range(1, n_high):
        line_copy(d).start()
    twin_copy(0, low).start()
    to_later(layer)

    for d in range(1, n_high):
        piece = lax.rem(high + n_high - d, n_high) * 2 + low
        remote(kv.at[ctx, piece], kv.at[ctx, piece], gz_s.at[d], gz_r.at[d],
               layer, ctx).wait_recv()
        twin_copy(d, low).start()
        to_later(piece)
    for d in range(n_high):
        twin_copy(d, 1 - low).wait_recv()
        to_later(lax.rem(high + n_high - d, n_high) * 2 + (1 - low))

    def block_of(j, which, g):
        part = kv[j, :, which, :, g * W : (g + 1) * W]
        if rows % 16:
            return part.astype(jnp.float32).reshape(n_layer * rows, W).astype(jnp.bfloat16)
        return part.reshape(n_layer * rows, W)

    def query_of(g):
        return jnp.concatenate(
            [q_ref[:, (g * GROUP + r) * W : (g * GROUP + r + 1) * W] for r in range(GROUP)], axis=0)

    peak[...] = jnp.full_like(peak, NEGATIVE_FILL)
    total[...] = jnp.zeros_like(total)
    att[...] = jnp.zeros_like(att)
    dqt[...] = jnp.zeros_like(dqt)

    for load in (q_load, *small_loads):
        load.wait()
    seg_q = seg_ref[pl.ds(ctx, 1), :]

    def score_block(i, carry):
        j = ctx - i

        if not isinstance(i, int):
            remote(kv.at[j], kv.at[j], gc_s.at[j], gc_r.at[j], layer, ctx).wait_recv()

        seg_k = jnp.transpose(
            jnp.broadcast_to(seg_ref[pl.ds(j, 1), :], (local, local)).astype(jnp.float32))
        same = seg_k == jnp.broadcast_to(seg_q, (local, local)).astype(jnp.float32)
        k_pos = j * local + lax.broadcasted_iota(jnp.int32, (local, local), 0)
        q_pos = ctx * local + lax.broadcasted_iota(jnp.int32, (local, local), 1)
        fill = jnp.where(same & (k_pos <= q_pos), 0.0, NEGATIVE_FILL)
        fill = jnp.concatenate([fill] * GROUP, axis=1)
        ahead = dot(block_of(j, 0, 0), query_of(0), 1, 1)
        for g in range(KEY_VALUE_HEADS):
            s = jnp.where(fill < 0.0, NEGATIVE_FILL, ahead * (LOG2_E * W ** -0.5))
            if g + 1 < KEY_VALUE_HEADS:
                ahead = dot(block_of(j, 0, g + 1), query_of(g + 1), 1, 1)
            top = jnp.maximum(peak[g], jnp.max(s, axis=0, keepdims=True))
            fade = jnp.exp2(peak[g] - top)
            p = jnp.exp2(s - top)
            score[j, g] = p
            tops[j, g] = top
            peak[g] = top
            total[g] = total[g] * fade + jnp.sum(p, axis=0, keepdims=True)
            att[g] = att[g] * fade + dot(block_of(j, 1, g), p.astype(jnp.bfloat16), 0, 0)
        return carry

    score_block(0, 0)

    head_load.wait()
    for k in range(classes):
        for h in range(QUERY_HEADS):
            row = head_ref[k : k + 1, h * W : (h + 1) * W]
            hb[k, h] = jnp.transpose(jnp.broadcast_to(row, (local, W)))

    lax.fori_loop(1, count, score_block, 0)

    logits = [jnp.zeros((1, local), jnp.float32) for _ in range(classes)]
    parts = []
    for g in range(KEY_VALUE_HEADS):
        inverse = 1.0 / total[g]
        total[g] = inverse
        att[g] = att[g] * inverse
        for r in range(GROUP):
            a = att[g, :, r * W : (r + 1) * W]
            part = [jnp.sum(hb[k, g * GROUP + r] * a, axis=0, keepdims=True)
                    for k in range(classes)]
            parts.append(part)
            logits = [x + y for x, y in zip(logits, part)]
    biggest = functools.reduce(jnp.maximum, logits)
    log_total = biggest + jnp.log(sum(jnp.exp(x - biggest) for x in logits))
    mask = mask_ref[...].astype(jnp.float32)
    hot = [(label_ref[...] == k).astype(jnp.float32) for k in range(classes)]
    loss_rows = mask * (log_total - sum(o * x for o, x in zip(hot, logits)))
    d_logits = [mask * (jnp.exp(x - log_total) - o) for o, x in zip(hot, logits)]

    for h in range(QUERY_HEADS):
        g, r = h // GROUP, h % GROUP
        cols = slice(r * W, (r + 1) * W)
        da = sum(hb[k, h] * d_logits[k] for k in range(classes))
        datt[g, :, cols] = da.astype(jnp.bfloat16)
        delta[g, :, cols] = sum(parts[h][k] * d_logits[k] for k in range(classes))
    for k in range(classes):
        rows_d[k : k + 1, :] = d_logits[k]
    rows_d[classes : classes + 1, :] = loss_rows

    def back_block(j, keep):
        ahead = dot(block_of(j, 1, 0), datt[0], 1, 0)
        for g in range(KEY_VALUE_HEADS):
            dp = ahead
            if g + 1 < KEY_VALUE_HEADS:
                ahead = dot(block_of(j, 1, g + 1), datt[g + 1], 1, 0)
            prob = score[j, g] * (total[g] * jnp.exp2(tops[j, g] - peak[g]))
            ds = (prob * ((dp - delta[g]) * W ** -0.5)).astype(jnp.bfloat16)
            cols = slice(g * W, (g + 1) * W)
            keep(1, cols, dot(prob.astype(jnp.bfloat16), datt[g], 1, 1))
            keep(0, cols, dot(ds, query_of(g), 1, 0))
            dqt[g] += dot(block_of(j, 0, g), ds, 0, 0)

    def earlier_block(j, carry):
        def keep(which, cols, value):
            send_ctx[j, :, which, :, cols] = value.reshape(n_layer, rows, W).astype(jnp.bfloat16)

        back_block(j, keep)
        for d in range(n_high):
            part = pl.ds(lax.rem(high + 1 + d, n_high) * 2, 2)
            remote(send_ctx.at[j, part], recv_ctx.at[ctx, part], rc_s.at[j],
                   rc_r.at[ctx, d], layer, j).start()
        return carry

    lax.fori_loop(first, ctx, earlier_block, 0)

    def keep_own(which, cols, value):
        grad[:, which, :, cols] = value.reshape(n_layer, rows, W)

    back_block(ctx, keep_own)

    def side_work():
        stacked = jnp.concatenate(
            [rows_d[0:classes, :], jnp.zeros((STAT_ROWS - classes, local), jnp.float32)], axis=0)
        for h in range(QUERY_HEADS):
            g, r = h // GROUP, h % GROUP
            stats[ctx, :, h * W : (h + 1) * W] = dot(
                stacked, att[g, :, r * W : (r + 1) * W], 1, 1, HIGH)
        stats[ctx, classes : classes + 1, 0:local] = rows_d[classes : classes + 1, :]
        for d in range(1, n_ctx):
            remote(stats.at[ctx], stats.at[ctx], st_s.at[d], st_r.at[d],
                   layer, lax.rem(ctx + d, n_ctx)).start()
        for h in range(QUERY_HEADS):
            g, r = h // GROUP, h % GROUP
            dq_ref[:, h * W : (h + 1) * W] = jnp.transpose(dqt[g, :, r * W : (r + 1) * W])

    def place(d):
        return lax.rem(high + 1 + d, n_high)

    def x_copy(d):
        return remote(send_x.at[d], recv_x.at[d], rx_s.at[d], rx_r.at[d], twin, ctx)

    def z_copy(d):
        return remote(send_z.at[d], recv_z.at[d], rz_s.at[d], rz_r.at[d],
                      place(d) * 2 + low, ctx)

    def x_stage(d):
        part = pl.ds(place(d) * 2, 2)

        def one(i, carry):
            remote(send_ctx.at[i, part], recv_ctx.at[i, part], rc_s.at[i], rc_r.at[i, d],
                   layer, ctx).wait_recv()
            grad[part] = grad[part] + recv_ctx[i, part].astype(jnp.float32)
            return carry

        lax.fori_loop(ctx + 1, end, one, 0)
        send_x[d] = grad[place(d) * 2 + (1 - low)].astype(jnp.bfloat16)
        x_copy(d).start()

    def z_stage(d):
        x_copy(d).wait_recv()
        value = grad[place(d) * 2 + low] + recv_x[d].astype(jnp.float32)
        if d < n_high - 1:
            send_z[d] = value.astype(jnp.bfloat16)
            z_copy(d).start()
        else:
            mine[...] = value

    @pl.when(ctx < end - 1)
    def _():
        side_work()
        for d in range(n_high):
            x_stage(d)
            if d:
                z_stage(d - 1)
        z_stage(n_high - 1)

    @pl.when(ctx == end - 1)
    def _():
        for d in range(n_high):
            x_stage(d)
        side_work()
        for d in range(n_high):
            z_stage(d)

    for d in range(1, n_ctx):
        origin = lax.rem(ctx + n_ctx - d, n_ctx)
        remote(stats.at[origin], stats.at[origin], st_s.at[d], st_r.at[d],
               layer, ctx).wait_recv()
    whole = stats[0]
    for j in range(1, n_ctx):
        whole = whole + stats[j]
    hg_ref[...] = whole[0:classes]
    loss_ref[0] = jnp.sum(whole[classes : classes + 1, 0:local]) * (1.0 / (local * n_ctx))

    result = mine[...]
    for d in range(n_high - 1):
        z_copy(d).wait_recv()
        result = result + recv_z[d].astype(jnp.float32)
    gk_ref[...] = result[0]
    gv_ref[...] = result[1]

    for d in range(1, n_high):
        line_copy(d).wait_send()
    for d in range(n_high - 1):
        z_copy(d).wait_send()
    for d in range(n_high):
        twin_copy(d, low).wait_send()
        x_copy(d).wait_send()
    for d in range(1, n_ctx):
        remote(stats.at[ctx], stats.at[ctx], st_s.at[d], st_r.at[d],
               layer, lax.rem(ctx + d, n_ctx)).wait_send()

    def sent_later(to, carry):
        remote(kv.at[ctx], kv.at[ctx], gc_s.at[to], gc_r.at[ctx], layer, to).wait_send()
        return carry

    lax.fori_loop(ctx + 1, end, sent_later, 0)

    def sent_back(j, carry):
        remote(send_ctx.at[j], recv_ctx.at[ctx], rc_s.at[j], rc_r.at[ctx, 0], layer, j).wait_send()
        return carry

    lax.fori_loop(first, ctx, sent_back, 0)


def write_out(*refs):
    copies = [pltpu.make_async_copy(refs[i], refs[4 + i], refs[8].at[i]) for i in range(4)]
    for copy in copies:
        copy.start()
    for copy in copies:
        copy.wait()


def per_device(queries, keys, values, head, segments, label_mask, labels):
    n_layer, n_ctx = lax.axis_size("layer"), lax.axis_size("ctx")
    local, width = queries.shape[1:]
    rows, kv_width = keys.shape
    classes = head.shape[2]
    n_high = n_layer // 2
    G, W, T = KEY_VALUE_HEADS, HEAD_WIDTH, GROUP * local
    vmem = pl.BlockSpec(memory_space=pltpu.VMEM)
    bf, f32 = jnp.bfloat16, jnp.float32
    dma = pltpu.SemaphoreType.DMA
    results = ((local, width), (rows, kv_width), (rows, kv_width), (classes, width))
    results_bytes = 4 * sum(a * b for a, b in results)
    loss, *computed = pl.pallas_call(
        functools.partial(kernel, n_layer, n_ctx),
        out_shape=(
            jax.ShapeDtypeStruct((1,), f32),
            *(pltpu.VMEM(shape, f32) for shape in results),
        ),
        in_specs=[pl.BlockSpec(memory_space=pltpu.HBM)] * 7,
        out_specs=(pl.BlockSpec(memory_space=pltpu.SMEM), vmem, vmem, vmem, vmem),
        scratch_shapes=[
            pltpu.VMEM((local, width), bf),
            pltpu.VMEM((classes, width), f32),
            pltpu.VMEM((n_ctx, local), jnp.int32),
            pltpu.VMEM((1, local), jnp.int32),
            pltpu.VMEM((1, local), jnp.int32),
            dma((7,)),
            pltpu.VMEM((n_ctx, n_layer, 2, rows, kv_width), bf),
            pltpu.VMEM((n_ctx, G, local, T), f32),
            pltpu.VMEM((classes, QUERY_HEADS, W, local), f32),
            pltpu.VMEM((G, 1, T), f32),
            pltpu.VMEM((n_ctx, G, 1, T), f32),
            pltpu.VMEM((G, 1, T), f32),
            pltpu.VMEM((G, W, T), f32),
            pltpu.VMEM((G, W, T), bf),
            pltpu.VMEM((G, 1, T), f32),
            pltpu.VMEM((G, W, T), f32),
            pltpu.VMEM((n_layer, 2, rows, kv_width), f32),
            pltpu.VMEM((2, rows, kv_width), f32),
            pltpu.VMEM((STAT_ROWS, local), f32),
            pltpu.VMEM((n_ctx, STAT_ROWS, width), f32),
            pltpu.VMEM((n_ctx, n_layer, 2, rows, kv_width), bf),
            pltpu.VMEM((n_ctx, n_layer, 2, rows, kv_width), bf),
            pltpu.VMEM((n_high, 2, rows, kv_width), bf),
            pltpu.VMEM((n_high, 2, rows, kv_width), bf),
            pltpu.VMEM((n_high, 2, rows, kv_width), bf),
            pltpu.VMEM((n_high, 2, rows, kv_width), bf),
            dma((n_high,)), dma((n_high,)), dma((n_high,)), dma((n_high,)),
            dma((n_ctx,)), dma((n_ctx,)), dma((n_ctx,)), dma((n_ctx,)),
            dma((n_ctx,)), dma((n_ctx, n_high)), dma((n_high,)), dma((n_high,)),
            dma((n_high,)), dma((n_high,)),
        ],
        compiler_params=pltpu.CompilerParams(
            collective_id=0, has_side_effects=True, vmem_limit_bytes=64 * 1024 * 1024 - results_bytes - 256 * 1024),
    )(
        queries[0], keys, values, jnp.swapaxes(head[0], 0, 1),
        segments.reshape(n_ctx, local), label_mask[None], labels[None],
    )
    hbm = pl.BlockSpec(memory_space=pltpu.HBM)
    dq, gk, gv, hg = pl.pallas_call(
        write_out,
        out_shape=tuple(jax.ShapeDtypeStruct(shape, f32) for shape in results),
        in_specs=[vmem] * 4,
        out_specs=(hbm,) * 4,
        scratch_shapes=[dma((4,))],
    )(*computed)
    return loss, dq[None], gk, gv, jnp.swapaxes(hg, 0, 1)[None]


def solution(mesh):
    return jax.shard_map(
        per_device,
        mesh=mesh,
        in_specs=(
            P("layer", "ctx", None),
            P(("ctx", "layer"), None),
            P(("ctx", "layer"), None),
            P("layer", None, None),
            P(),
            P("ctx"),
            P("ctx"),
        ),
        out_specs=(
            P("layer"),
            P("layer", "ctx", None),
            P(("ctx", "layer"), None),
            P(("ctx", "layer"), None),
            P("layer", None, None),
        ),
        check_vma=False,
    )
```

```python
import functools

import jax
import jax.numpy as jnp
from jax import lax
from jax.experimental import pallas as pl
from jax.experimental.pallas import tpu as pltpu
from jax.sharding import PartitionSpec as P

QUERY_HEADS = 12
KEY_VALUE_HEADS = 4
HEAD_WIDTH = 128

GROUP = QUERY_HEADS // KEY_VALUE_HEADS
LOG2_E = 1.4426950408889634
NEGATIVE_FILL = -1e30
HIGH = lax.Precision.HIGHEST
MESH = pl.DeviceIdType.MESH
STAT_ROWS = 8


def dot(a, b, a_dim, b_dim, precision=None):
    return lax.dot_general(
        a, b, (((a_dim,), (b_dim,)), ((), ())), precision=precision,
        preferred_element_type=jnp.float32,
    )


def kernel(
    n_layer, n_ctx, q_in, k_in, v_in, head_in, seg_in, mask_in, label_in,
    loss_ref, dq_ref, gk_ref, gv_ref, hg_ref,
    q_ref, head_ref, seg_ref, mask_ref, label_ref, in_sem,
    kv, score, hb, peak, tops, total, att, datt, delta, dqt, grad, mine, rows_d, stats,
    send_ctx, recv_ctx, send_x, recv_x, send_z, recv_z,
    gz_s, gz_r, gx_s, gx_r, gc_s, gc_r, st_s, st_r, rc_s, rc_r, rx_s, rx_r, rz_s, rz_r,
):
    W = HEAD_WIDTH
    local = q_ref.shape[0]
    rows = k_in.shape[0]
    classes = head_ref.shape[0]
    n_high = n_layer // 2
    layer, ctx = lax.axis_index("layer"), lax.axis_index("ctx")
    high, low = layer // 2, layer % 2
    twin = high * 2 + (1 - low)
    tail = (3 * n_ctx) // 4
    in_tail = (ctx >= tail).astype(jnp.int32)
    first = in_tail * tail
    end = tail + in_tail * (n_ctx - tail)
    count = ctx - first + 1

    def remote(src, dst, s, r, to_layer, to_ctx):
        return pltpu.make_async_remote_copy(
            src_ref=src, dst_ref=dst, send_sem=s, recv_sem=r,
            device_id=(to_layer, to_ctx), device_id_type=MESH,
        )

    k_load, v_load, head_load, q_load, *small_loads = [
        pltpu.make_async_copy(src, dst, in_sem.at[i])
        for i, (src, dst) in enumerate([
            (k_in, kv.at[ctx, layer, 0]), (v_in, kv.at[ctx, layer, 1]), (head_in, head_ref),
            (q_in, q_ref), (seg_in, seg_ref), (mask_in, mask_ref), (label_in, label_ref)])
    ]
    for load in (k_load, v_load, head_load, q_load, *small_loads):
        load.start()

    barrier = pltpu.get_barrier_semaphore()
    for d in range(1, n_high):
        pl.semaphore_signal(
            barrier, inc=1, device_id=(lax.rem(high + d, n_high) * 2 + low, ctx),
            device_id_type=MESH)
    pl.semaphore_signal(barrier, inc=1, device_id=(twin, ctx), device_id_type=MESH)
    for d in range(1, n_ctx):
        pl.semaphore_signal(
            barrier, inc=1, device_id=(layer, lax.rem(ctx + d, n_ctx)), device_id_type=MESH)
    k_load.wait()
    v_load.wait()
    pl.semaphore_wait(barrier, n_high + n_ctx - 1)

    def to_later(piece):
        def one(to, carry):
            remote(kv.at[ctx, piece], kv.at[ctx, piece], gc_s.at[to], gc_r.at[ctx],
                   layer, to).start()
            return carry
        lax.fori_loop(ctx + 1, end, one, 0)

    def line_copy(d):
        return remote(kv.at[ctx, layer], kv.at[ctx, layer], gz_s.at[d], gz_r.at[d],
                      lax.rem(high + d, n_high) * 2 + low, ctx)

    def twin_copy(d, side):
        piece = lax.rem(high + n_high - d, n_high) * 2 + side
        return remote(kv.at[ctx, piece], kv.at[ctx, piece], gx_s.at[d], gx_r.at[d], twin, ctx)

    for d in range(1, n_high):
        line_copy(d).start()
    twin_copy(0, low).start()
    to_later(layer)

    for d in range(1, n_high):
        piece = lax.rem(high + n_high - d, n_high) * 2 + low
        remote(kv.at[ctx, piece], kv.at[ctx, piece], gz_s.at[d], gz_r.at[d],
               layer, ctx).wait_recv()
        twin_copy(d, low).start()
        to_later(piece)
    for d in range(n_high):
        twin_copy(d, 1 - low).wait_recv()
        to_later(lax.rem(high + n_high - d, n_high) * 2 + (1 - low))

    def block_of(j, which, g):
        part = kv[j, :, which, :, g * W : (g + 1) * W]
        if rows % 16:
            return part.astype(jnp.float32).reshape(n_layer * rows, W).astype(jnp.bfloat16)
        return part.reshape(n_layer * rows, W)

    def query_of(g):
        return jnp.concatenate(
            [q_ref[:, (g * GROUP + r) * W : (g * GROUP + r + 1) * W] for r in range(GROUP)], axis=0)

    peak[...] = jnp.full_like(peak, NEGATIVE_FILL)
    total[...] = jnp.zeros_like(total)
    att[...] = jnp.zeros_like(att)
    dqt[...] = jnp.zeros_like(dqt)

    for load in (q_load, *small_loads):
        load.wait()
    seg_q = seg_ref[pl.ds(ctx, 1), :]

    def score_block(i, carry):
        j = ctx - i

        if not isinstance(i, int):
            remote(kv.at[j], kv.at[j], gc_s.at[j], gc_r.at[j], layer, ctx).wait_recv()

        seg_k = jnp.transpose(
            jnp.broadcast_to(seg_ref[pl.ds(j, 1), :], (local, local)).astype(jnp.float32))
        same = seg_k == jnp.broadcast_to(seg_q, (local, local)).astype(jnp.float32)
        k_pos = j * local + lax.broadcasted_iota(jnp.int32, (local, local), 0)
        q_pos = ctx * local + lax.broadcasted_iota(jnp.int32, (local, local), 1)
        fill = jnp.where(same & (k_pos <= q_pos), 0.0, NEGATIVE_FILL)
        fill = jnp.concatenate([fill] * GROUP, axis=1)
        ahead = dot(block_of(j, 0, 0), query_of(0), 1, 1)
        for g in range(KEY_VALUE_HEADS):
            s = jnp.where(fill < 0.0, NEGATIVE_FILL, ahead * (LOG2_E * W ** -0.5))
            if g + 1 < KEY_VALUE_HEADS:
                ahead = dot(block_of(j, 0, g + 1), query_of(g + 1), 1, 1)
            top = jnp.maximum(peak[g], jnp.max(s, axis=0, keepdims=True))
            fade = jnp.exp2(peak[g] - top)
            p = jnp.exp2(s - top)
            score[j, g] = p
            tops[j, g] = top
            peak[g] = top
            total[g] = total[g] * fade + jnp.sum(p, axis=0, keepdims=True)
            att[g] = att[g] * fade + dot(block_of(j, 1, g), p.astype(jnp.bfloat16), 0, 0)
        return carry

    score_block(0, 0)

    head_load.wait()
    for k in range(classes):
        for h in range(QUERY_HEADS):
            row = head_ref[k : k + 1, h * W : (h + 1) * W]
            hb[k, h] = jnp.transpose(jnp.broadcast_to(row, (local, W)))

    lax.fori_loop(1, count, score_block, 0)

    logits = [jnp.zeros((1, local), jnp.float32) for _ in range(classes)]
    parts = []
    for g in range(KEY_VALUE_HEADS):
        inverse = 1.0 / total[g]
        total[g] = inverse
        att[g] = att[g] * inverse
        for r in range(GROUP):
            a = att[g, :, r * W : (r + 1) * W]
            part = [jnp.sum(hb[k, g * GROUP + r] * a, axis=0, keepdims=True)
                    for k in range(classes)]
            parts.append(part)
            logits = [x + y for x, y in zip(logits, part)]
    biggest = functools.reduce(jnp.maximum, logits)
    log_total = biggest + jnp.log(sum(jnp.exp(x - biggest) for x in logits))
    mask = mask_ref[...].astype(jnp.float32)
    hot = [(label_ref[...] == k).astype(jnp.float32) for k in range(classes)]
    loss_rows = mask * (log_total - sum(o * x for o, x in zip(hot, logits)))
    d_logits = [mask * (jnp.exp(x - log_total) - o) for o, x in zip(hot, logits)]

    for h in range(QUERY_HEADS):
        g, r = h // GROUP, h % GROUP
        cols = slice(r * W, (r + 1) * W)
        da = sum(hb[k, h] * d_logits[k] for k in range(classes))
        datt[g, :, cols] = da.astype(jnp.bfloat16)
        delta[g, :, cols] = sum(parts[h][k] * d_logits[k] for k in range(classes))
    for k in range(classes):
        rows_d[k : k + 1, :] = d_logits[k]
    rows_d[classes : classes + 1, :] = loss_rows

    def back_block(j, keep):
        ahead = dot(block_of(j, 1, 0), datt[0], 1, 0)
        for g in range(KEY_VALUE_HEADS):
            dp = ahead
            if g + 1 < KEY_VALUE_HEADS:
                ahead = dot(block_of(j, 1, g + 1), datt[g + 1], 1, 0)
            prob = score[j, g] * (total[g] * jnp.exp2(tops[j, g] - peak[g]))
            ds = (prob * ((dp - delta[g]) * W ** -0.5)).astype(jnp.bfloat16)
            cols = slice(g * W, (g + 1) * W)
            keep(1, cols, dot(prob.astype(jnp.bfloat16), datt[g], 1, 1))
            keep(0, cols, dot(ds, query_of(g), 1, 0))
            dqt[g] += dot(block_of(j, 0, g), ds, 0, 0)

    def earlier_block(j, carry):
        def keep(which, cols, value):
            send_ctx[j, :, which, :, cols] = value.reshape(n_layer, rows, W).astype(jnp.bfloat16)

        back_block(j, keep)
        for d in range(n_high):
            part = pl.ds(lax.rem(high + 1 + d, n_high) * 2, 2)
            remote(send_ctx.at[j, part], recv_ctx.at[ctx, part], rc_s.at[j],
                   rc_r.at[ctx, d], layer, j).start()
        return carry

    lax.fori_loop(first, ctx, earlier_block, 0)

    def keep_own(which, cols, value):
        grad[:, which, :, cols] = value.reshape(n_layer, rows, W)

    back_block(ctx, keep_own)

    def side_work():
        stacked = jnp.concatenate(
            [rows_d[0:classes, :], jnp.zeros((STAT_ROWS - classes, local), jnp.float32)], axis=0)
        for h in range(QUERY_HEADS):
            g, r = h // GROUP, h % GROUP
            stats[ctx, :, h * W : (h + 1) * W] = dot(
                stacked, att[g, :, r * W : (r + 1) * W], 1, 1, HIGH)
        stats[ctx, classes : classes + 1, 0:local] = rows_d[classes : classes + 1, :]
        for d in range(1, n_ctx):
            remote(stats.at[ctx], stats.at[ctx], st_s.at[d], st_r.at[d],
                   layer, lax.rem(ctx + d, n_ctx)).start()
        for h in range(QUERY_HEADS):
            g, r = h // GROUP, h % GROUP
            dq_ref[:, h * W : (h + 1) * W] = jnp.transpose(dqt[g, :, r * W : (r + 1) * W])

    def place(d):
        return lax.rem(high + 1 + d, n_high)

    def x_copy(d):
        return remote(send_x.at[d], recv_x.at[d], rx_s.at[d], rx_r.at[d], twin, ctx)

    def z_copy(d):
        return remote(send_z.at[d], recv_z.at[d], rz_s.at[d], rz_r.at[d],
                      place(d) * 2 + low, ctx)

    def x_stage(d):
        part = pl.ds(place(d) * 2, 2)

        def one(i, carry):
            remote(send_ctx.at[i, part], recv_ctx.at[i, part], rc_s.at[i], rc_r.at[i, d],
                   layer, ctx).wait_recv()
            grad[part] = grad[part] + recv_ctx[i, part].astype(jnp.float32)
            return carry

        lax.fori_loop(ctx + 1, end, one, 0)
        send_x[d] = grad[place(d) * 2 + (1 - low)].astype(jnp.bfloat16)
        x_copy(d).start()

    def z_stage(d):
        x_copy(d).wait_recv()
        value = grad[place(d) * 2 + low] + recv_x[d].astype(jnp.float32)
        if d < n_high - 1:
            send_z[d] = value.astype(jnp.bfloat16)
            z_copy(d).start()
        else:
            mine[...] = value

    @pl.when(ctx < end - 1)
    def _():
        side_work()
        for d in range(n_high):
            x_stage(d)
            if d:
                z_stage(d - 1)
        z_stage(n_high - 1)

    @pl.when(ctx == end - 1)
    def _():
        for d in range(n_high):
            x_stage(d)
        side_work()
        for d in range(n_high):
            z_stage(d)

    for d in range(1, n_ctx):
        origin = lax.rem(ctx + n_ctx - d, n_ctx)
        remote(stats.at[origin], stats.at[origin], st_s.at[d], st_r.at[d],
               layer, ctx).wait_recv()
    whole = stats[0]
    for j in range(1, n_ctx):
        whole = whole + stats[j]
    hg_ref[...] = whole[0:classes]
    loss_ref[0] = jnp.sum(whole[classes : classes + 1, 0:local]) * (1.0 / (local * n_ctx))

    result = mine[...]
    for d in range(n_high - 1):
        z_copy(d).wait_recv()
        result = result + recv_z[d].astype(jnp.float32)
    gk_ref[...] = result[0]
    gv_ref[...] = result[1]

    for d in range(1, n_high):
        line_copy(d).wait_send()
    for d in range(n_high - 1):
        z_copy(d).wait_send()
    for d in range(n_high):
        twin_copy(d, low).wait_send()
        x_copy(d).wait_send()
    for d in range(1, n_ctx):
        remote(stats.at[ctx], stats.at[ctx], st_s.at[d], st_r.at[d],
               layer, lax.rem(ctx + d, n_ctx)).wait_send()

    def sent_later(to, carry):
        remote(kv.at[ctx], kv.at[ctx], gc_s.at[to], gc_r.at[ctx], layer, to).wait_send()
        return carry

    lax.fori_loop(ctx + 1, end, sent_later, 0)

    def sent_back(j, carry):
        remote(send_ctx.at[j], recv_ctx.at[ctx], rc_s.at[j], rc_r.at[ctx, 0], layer, j).wait_send()
        return carry

    lax.fori_loop(first, ctx, sent_back, 0)


def write_out(*refs):
    copies = [pltpu.make_async_copy(refs[i], refs[4 + i], refs[8].at[i]) for i in range(4)]
    for copy in copies:
        copy.start()
    for copy in copies:
        copy.wait()


def per_device(queries, keys, values, head, segments, label_mask, labels):
    n_layer, n_ctx = lax.axis_size("layer"), lax.axis_size("ctx")
    local, width = queries.shape[1:]
    rows, kv_width = keys.shape
    classes = head.shape[2]
    n_high = n_layer // 2
    G, W, T = KEY_VALUE_HEADS, HEAD_WIDTH, GROUP * local
    vmem = pl.BlockSpec(memory_space=pltpu.VMEM)
    bf, f32 = jnp.bfloat16, jnp.float32
    dma = pltpu.SemaphoreType.DMA
    results = ((local, width), (rows, kv_width), (rows, kv_width), (classes, width))
    results_bytes = 4 * sum(a * b for a, b in results)
    loss, *computed = pl.pallas_call(
        functools.partial(kernel, n_layer, n_ctx),
        out_shape=(
            jax.ShapeDtypeStruct((1,), f32),
            *(pltpu.VMEM(shape, f32) for shape in results),
        ),
        in_specs=[pl.BlockSpec(memory_space=pltpu.HBM)] * 7,
        out_specs=(pl.BlockSpec(memory_space=pltpu.SMEM), vmem, vmem, vmem, vmem),
        scratch_shapes=[
            pltpu.VMEM((local, width), bf),
            pltpu.VMEM((classes, width), f32),
            pltpu.VMEM((n_ctx, local), jnp.int32),
            pltpu.VMEM((1, local), jnp.int32),
            pltpu.VMEM((1, local), jnp.int32),
            dma((7,)),
            pltpu.VMEM((n_ctx, n_layer, 2, rows, kv_width), bf),
            pltpu.VMEM((n_ctx, G, local, T), f32),
            pltpu.VMEM((classes, QUERY_HEADS, W, local), f32),
            pltpu.VMEM((G, 1, T), f32),
            pltpu.VMEM((n_ctx, G, 1, T), f32),
            pltpu.VMEM((G, 1, T), f32),
            pltpu.VMEM((G, W, T), f32),
            pltpu.VMEM((G, W, T), bf),
            pltpu.VMEM((G, 1, T), f32),
            pltpu.VMEM((G, W, T), f32),
            pltpu.VMEM((n_layer, 2, rows, kv_width), f32),
            pltpu.VMEM((2, rows, kv_width), f32),
            pltpu.VMEM((STAT_ROWS, local), f32),
            pltpu.VMEM((n_ctx, STAT_ROWS, width), f32),
            pltpu.VMEM((n_ctx, n_layer, 2, rows, kv_width), bf),
            pltpu.VMEM((n_ctx, n_layer, 2, rows, kv_width), bf),
            pltpu.VMEM((n_high, 2, rows, kv_width), bf),
            pltpu.VMEM((n_high, 2, rows, kv_width), bf),
            pltpu.VMEM((n_high, 2, rows, kv_width), bf),
            pltpu.VMEM((n_high, 2, rows, kv_width), bf),
            dma((n_high,)), dma((n_high,)), dma((n_high,)), dma((n_high,)),
            dma((n_ctx,)), dma((n_ctx,)), dma((n_ctx,)), dma((n_ctx,)),
            dma((n_ctx,)), dma((n_ctx, n_high)), dma((n_high,)), dma((n_high,)),
            dma((n_high,)), dma((n_high,)),
        ],
        compiler_params=pltpu.CompilerParams(
            collective_id=0, has_side_effects=True, vmem_limit_bytes=64 * 1024 * 1024 - results_bytes - 256 * 1024),
    )(
        queries[0], keys, values, jnp.swapaxes(head[0], 0, 1),
        segments.reshape(n_ctx, local), label_mask[None], labels[None],
    )
    hbm = pl.BlockSpec(memory_space=pltpu.HBM)
    dq, gk, gv, hg = pl.pallas_call(
        write_out,
        out_shape=tuple(jax.ShapeDtypeStruct(shape, f32) for shape in results),
        in_specs=[vmem] * 4,
        out_specs=(hbm,) * 4,
        scratch_shapes=[dma((4,))],
        compiler_params=pltpu.CompilerParams(vmem_limit_bytes=2 * results_bytes),
    )(*computed)
    return loss, dq[None], gk, gv, jnp.swapaxes(hg, 0, 1)[None]


def solution(mesh):
    return jax.shard_map(
        per_device,
        mesh=mesh,
        in_specs=(
            P("layer", "ctx", None),
            P(("ctx", "layer"), None),
            P(("ctx", "layer"), None),
            P("layer", None, None),
            P(),
            P("ctx"),
            P("ctx"),
        ),
        out_specs=(
            P("layer"),
            P("layer", "ctx", None),
            P(("ctx", "layer"), None),
            P(("ctx", "layer"), None),
            P("layer", None, None),
        ),
        check_vma=False,
    )
```

```python
import functools

import jax
import jax.numpy as jnp
from jax import lax
from jax.experimental import pallas as pl
from jax.experimental.pallas import tpu as pltpu
from jax.sharding import PartitionSpec as P

QUERY_HEADS = 12
KEY_VALUE_HEADS = 4
HEAD_WIDTH = 128

GROUP = QUERY_HEADS // KEY_VALUE_HEADS
LOG2_E = 1.4426950408889634
NEGATIVE_FILL = -1e30
HIGH = lax.Precision.HIGHEST
MESH = pl.DeviceIdType.MESH
STAT_ROWS = 8


def dot(a, b, a_dim, b_dim, precision=None):
    return lax.dot_general(
        a, b, (((a_dim,), (b_dim,)), ((), ())), precision=precision,
        preferred_element_type=jnp.float32,
    )


def kernel(
    n_layer, n_ctx, q_in, k_in, v_in, head_in, seg_in, mask_in, label_in,
    loss_ref, dq_ref, gk_ref, gv_ref, hg_ref,
    q_ref, head_ref, seg_ref, mask_ref, label_ref, in_sem,
    kv, score, hb, peak, tops, total, att, datt, delta, dqt, grad, mine, rows_d, stats,
    send_ctx, recv_ctx, send_x, recv_x, send_z, recv_z, recv_half, send_half, sum_half,
    gz_s, gz_r, gx_s, gx_r, gc_s, gc_r, st_s, st_r, rc_s, rc_r, rx_s, rx_r, rz_s, rz_r,
    gl_s, gl_r, gf_s, gf_r, tw_s, tw_r, rh_s, rh_r,
):
    W = HEAD_WIDTH
    local = q_ref.shape[0]
    rows = k_in.shape[0]
    classes = head_ref.shape[0]
    n_high = n_layer // 2
    layer, ctx = lax.axis_index("layer"), lax.axis_index("ctx")
    high, low = layer // 2, layer % 2
    twin = high * 2 + (1 - low)
    tail = (3 * n_ctx) // 4
    in_tail = (ctx >= tail).astype(jnp.int32)
    first = in_tail * tail
    end = tail + in_tail * (n_ctx - tail)
    count = ctx - first + 1
    even = ((ctx % 2) == 0).astype(jnp.int32)
    split = even * jnp.minimum(ctx + 2, end) + (1 - even) * end

    def halved(j):
        return ((j % 2) == 0) & (ctx - j >= 2)

    def remote(src, dst, s, r, to_layer, to_ctx):
        return pltpu.make_async_remote_copy(
            src_ref=src, dst_ref=dst, send_sem=s, recv_sem=r,
            device_id=(to_layer, to_ctx), device_id_type=MESH,
        )

    k_load, v_load, head_load, q_load, *small_loads = [
        pltpu.make_async_copy(src, dst, in_sem.at[i])
        for i, (src, dst) in enumerate([
            (k_in, kv.at[ctx, layer, 0]), (v_in, kv.at[ctx, layer, 1]), (head_in, head_ref),
            (q_in, q_ref), (seg_in, seg_ref), (mask_in, mask_ref), (label_in, label_ref)])
    ]
    for load in (k_load, v_load, head_load, q_load, *small_loads):
        load.start()

    barrier = pltpu.get_barrier_semaphore()
    for d in range(1, n_high):
        pl.semaphore_signal(
            barrier, inc=1, device_id=(lax.rem(high + d, n_high) * 2 + low, ctx),
            device_id_type=MESH)
    pl.semaphore_signal(barrier, inc=1, device_id=(twin, ctx), device_id_type=MESH)
    for d in range(1, n_ctx):
        pl.semaphore_signal(
            barrier, inc=1, device_id=(layer, lax.rem(ctx + d, n_ctx)), device_id_type=MESH)
    k_load.wait()
    v_load.wait()
    pl.semaphore_wait(barrier, n_high + n_ctx - 1)

    def to_later(piece, d=None):
        def whole(to, carry):
            remote(kv.at[ctx, piece], kv.at[ctx, piece], gc_s.at[to], gc_r.at[ctx],
                   layer, to).start()
            return carry

        def half(to, carry):
            half_copy(to, d).start()
            return carry

        lax.fori_loop(ctx + 1, split, whole, 0)
        if d is not None:
            lax.fori_loop(split, end, half, 0)

    def line_piece(d, side):
        return lax.rem(high + n_high - d, n_high) * 2 + side

    def half_copy(to, d):
        piece = line_piece(d, low)
        return remote(kv.at[ctx, piece], kv.at[ctx, piece], gl_s.at[to, d], gl_r.at[ctx, d],
                      layer, to)

    def forward_copy(j, d, side):
        piece = line_piece(d, side)
        return remote(kv.at[j, piece], kv.at[j, piece], gf_s.at[j, d], gf_r.at[j, d], twin, ctx)

    def line_copy(d):
        return remote(kv.at[ctx, layer], kv.at[ctx, layer], gz_s.at[d], gz_r.at[d],
                      lax.rem(high + d, n_high) * 2 + low, ctx)

    def twin_copy(d, side):
        piece = lax.rem(high + n_high - d, n_high) * 2 + side
        return remote(kv.at[ctx, piece], kv.at[ctx, piece], gx_s.at[d], gx_r.at[d], twin, ctx)

    for d in range(1, n_high):
        line_copy(d).start()
    twin_copy(0, low).start()
    to_later(layer, 0)

    for d in range(1, n_high):
        piece = lax.rem(high + n_high - d, n_high) * 2 + low
        remote(kv.at[ctx, piece], kv.at[ctx, piece], gz_s.at[d], gz_r.at[d],
               layer, ctx).wait_recv()
        twin_copy(d, low).start()
        to_later(piece, d)
    for d in range(n_high):
        twin_copy(d, 1 - low).wait_recv()
        to_later(lax.rem(high + n_high - d, n_high) * 2 + (1 - low))

    def block_of(j, which, g):
        part = kv[j, :, which, :, g * W : (g + 1) * W]
        if rows % 16:
            return part.astype(jnp.float32).reshape(n_layer * rows, W).astype(jnp.bfloat16)
        return part.reshape(n_layer * rows, W)

    def query_of(g):
        return jnp.concatenate(
            [q_ref[:, (g * GROUP + r) * W : (g * GROUP + r + 1) * W] for r in range(GROUP)], axis=0)

    peak[...] = jnp.full_like(peak, NEGATIVE_FILL)
    total[...] = jnp.zeros_like(total)
    att[...] = jnp.zeros_like(att)
    dqt[...] = jnp.zeros_like(dqt)

    for load in (q_load, *small_loads):
        load.wait()
    seg_q = seg_ref[pl.ds(ctx, 1), :]

    def score_block(i, carry):
        j = ctx - i

        if not isinstance(i, int):
            @pl.when(halved(j))
            def _():
                for d in range(n_high):
                    forward_copy(j, d, 1 - low).wait_recv()

            @pl.when(jnp.logical_not(halved(j)))
            def _():
                remote(kv.at[j], kv.at[j], gc_s.at[j], gc_r.at[j], layer, ctx).wait_recv()

        seg_k = jnp.transpose(
            jnp.broadcast_to(seg_ref[pl.ds(j, 1), :], (local, local)).astype(jnp.float32))
        same = seg_k == jnp.broadcast_to(seg_q, (local, local)).astype(jnp.float32)
        k_pos = j * local + lax.broadcasted_iota(jnp.int32, (local, local), 0)
        q_pos = ctx * local + lax.broadcasted_iota(jnp.int32, (local, local), 1)
        fill = jnp.where(same & (k_pos <= q_pos), 0.0, NEGATIVE_FILL)
        fill = jnp.concatenate([fill] * GROUP, axis=1)
        ahead = dot(block_of(j, 0, 0), query_of(0), 1, 1)
        for g in range(KEY_VALUE_HEADS):
            s = jnp.where(fill < 0.0, NEGATIVE_FILL, ahead * (LOG2_E * W ** -0.5))
            if g + 1 < KEY_VALUE_HEADS:
                ahead = dot(block_of(j, 0, g + 1), query_of(g + 1), 1, 1)
            top = jnp.maximum(peak[g], jnp.max(s, axis=0, keepdims=True))
            fade = jnp.exp2(peak[g] - top)
            p = jnp.exp2(s - top)
            score[j, g] = p
            tops[j, g] = top
            peak[g] = top
            total[g] = total[g] * fade + jnp.sum(p, axis=0, keepdims=True)
            att[g] = att[g] * fade + dot(block_of(j, 1, g), p.astype(jnp.bfloat16), 0, 0)
        return carry

    score_block(0, 0)

    def pass_on(j, carry):
        @pl.when(halved(j))
        def _():
            for d in range(n_high):
                piece = line_piece(d, low)
                remote(kv.at[j, piece], kv.at[j, piece], gl_s.at[j, d], gl_r.at[j, d],
                       layer, ctx).wait_recv()
                forward_copy(j, d, low).start()
        return carry

    lax.fori_loop(first, ctx, pass_on, 0)

    head_load.wait()
    for k in range(classes):
        for h in range(QUERY_HEADS):
            row = head_ref[k : k + 1, h * W : (h + 1) * W]
            hb[k, h] = jnp.transpose(jnp.broadcast_to(row, (local, W)))

    lax.fori_loop(1, count, score_block, 0)

    logits = [jnp.zeros((1, local), jnp.float32) for _ in range(classes)]
    parts = []
    for g in range(KEY_VALUE_HEADS):
        inverse = 1.0 / total[g]
        total[g] = inverse
        att[g] = att[g] * inverse
        for r in range(GROUP):
            a = att[g, :, r * W : (r + 1) * W]
            part = [jnp.sum(hb[k, g * GROUP + r] * a, axis=0, keepdims=True)
                    for k in range(classes)]
            parts.append(part)
            logits = [x + y for x, y in zip(logits, part)]
    biggest = functools.reduce(jnp.maximum, logits)
    log_total = biggest + jnp.log(sum(jnp.exp(x - biggest) for x in logits))
    mask = mask_ref[...].astype(jnp.float32)
    hot = [(label_ref[...] == k).astype(jnp.float32) for k in range(classes)]
    loss_rows = mask * (log_total - sum(o * x for o, x in zip(hot, logits)))
    d_logits = [mask * (jnp.exp(x - log_total) - o) for o, x in zip(hot, logits)]

    for h in range(QUERY_HEADS):
        g, r = h // GROUP, h % GROUP
        cols = slice(r * W, (r + 1) * W)
        da = sum(hb[k, h] * d_logits[k] for k in range(classes))
        datt[g, :, cols] = da.astype(jnp.bfloat16)
        delta[g, :, cols] = sum(parts[h][k] * d_logits[k] for k in range(classes))
    for k in range(classes):
        rows_d[k : k + 1, :] = d_logits[k]
    rows_d[classes : classes + 1, :] = loss_rows

    def back_block(j, keep):
        ahead = dot(block_of(j, 1, 0), datt[0], 1, 0)
        for g in range(KEY_VALUE_HEADS):
            dp = ahead
            if g + 1 < KEY_VALUE_HEADS:
                ahead = dot(block_of(j, 1, g + 1), datt[g + 1], 1, 0)
            prob = score[j, g] * (total[g] * jnp.exp2(tops[j, g] - peak[g]))
            ds = (prob * ((dp - delta[g]) * W ** -0.5)).astype(jnp.bfloat16)
            cols = slice(g * W, (g + 1) * W)
            keep(1, cols, dot(prob.astype(jnp.bfloat16), datt[g], 1, 1))
            keep(0, cols, dot(ds, query_of(g), 1, 0))
            dqt[g] += dot(block_of(j, 0, g), ds, 0, 0)

    def place(d):
        return lax.rem(high + 1 + d, n_high)

    def twin_half(j, d):
        return remote(send_ctx.at[j, place(d) * 2 + (1 - low)], recv_half.at[j, d],
                      tw_s.at[j, d], tw_r.at[j, d], twin, ctx)

    def half_sum(j, d):
        return remote(send_half.at[j, d], sum_half.at[ctx, d], rh_s.at[j, d], rh_r.at[ctx, d],
                      layer, j)

    def earlier_block(i, carry):
        j = ctx - 1 - i

        def keep(which, cols, value):
            send_ctx[j, :, which, :, cols] = value.reshape(n_layer, rows, W).astype(jnp.bfloat16)

        back_block(j, keep)

        @pl.when(halved(j))
        def _():
            for d in range(n_high):
                twin_half(j, d).start()

        @pl.when(jnp.logical_not(halved(j)))
        def _():
            for d in range(n_high):
                part = pl.ds(place(d) * 2, 2)
                remote(send_ctx.at[j, part], recv_ctx.at[ctx, part], rc_s.at[j],
                       rc_r.at[ctx, d], layer, j).start()
        return carry

    lax.fori_loop(0, count - 1, earlier_block, 0)

    def keep_own(which, cols, value):
        grad[:, which, :, cols] = value.reshape(n_layer, rows, W)

    back_block(ctx, keep_own)

    def add_halves(j, carry):
        @pl.when(halved(j))
        def _():
            for d in range(n_high):
                twin_half(j, d).wait_recv()
                send_half[j, d] = (
                    send_ctx[j, place(d) * 2 + low].astype(jnp.float32)
                    + recv_half[j, d].astype(jnp.float32)).astype(jnp.bfloat16)
                half_sum(j, d).start()
        return carry

    lax.fori_loop(first, ctx, add_halves, 0)

    def side_work():
        stacked = jnp.concatenate(
            [rows_d[0:classes, :], jnp.zeros((STAT_ROWS - classes, local), jnp.float32)], axis=0)
        for h in range(QUERY_HEADS):
            g, r = h // GROUP, h % GROUP
            stats[ctx, :, h * W : (h + 1) * W] = dot(
                stacked, att[g, :, r * W : (r + 1) * W], 1, 1, HIGH)
        stats[ctx, classes : classes + 1, 0:local] = rows_d[classes : classes + 1, :]
        for d in range(1, n_ctx):
            remote(stats.at[ctx], stats.at[ctx], st_s.at[d], st_r.at[d],
                   layer, lax.rem(ctx + d, n_ctx)).start()
        for h in range(QUERY_HEADS):
            g, r = h // GROUP, h % GROUP
            dq_ref[:, h * W : (h + 1) * W] = jnp.transpose(dqt[g, :, r * W : (r + 1) * W])

    def x_copy(d):
        return remote(send_x.at[d], recv_x.at[d], rx_s.at[d], rx_r.at[d], twin, ctx)

    def z_copy(d):
        return remote(send_z.at[d], recv_z.at[d], rz_s.at[d], rz_r.at[d],
                      place(d) * 2 + low, ctx)

    def x_stage(d):
        part = pl.ds(place(d) * 2, 2)

        def one(i, carry):
            remote(send_ctx.at[i, part], recv_ctx.at[i, part], rc_s.at[i], rc_r.at[i, d],
                   layer, ctx).wait_recv()
            grad[part] = grad[part] + recv_ctx[i, part].astype(jnp.float32)
            return carry

        lax.fori_loop(ctx + 1, split, one, 0)
        send_x[d] = grad[place(d) * 2 + (1 - low)].astype(jnp.bfloat16)
        x_copy(d).start()

    def z_stage(d):
        x_copy(d).wait_recv()
        own = place(d) * 2 + low

        def one(i, carry):
            remote(send_half.at[i, d], sum_half.at[i, d], rh_s.at[i, d], rh_r.at[i, d],
                   layer, ctx).wait_recv()
            grad[own] = grad[own] + sum_half[i, d].astype(jnp.float32)
            return carry

        lax.fori_loop(split, end, one, 0)
        value = grad[own] + recv_x[d].astype(jnp.float32)
        if d < n_high - 1:
            send_z[d] = value.astype(jnp.bfloat16)
            z_copy(d).start()
        else:
            mine[...] = value

    waits = (ctx < end - 1) & (split == end)

    @pl.when(waits)
    def _():
        side_work()
        for d in range(n_high):
            x_stage(d)
            if d:
                z_stage(d - 1)
        z_stage(n_high - 1)

    @pl.when(jnp.logical_not(waits))
    def _():
        for d in range(n_high):
            x_stage(d)
        side_work()
        for d in range(n_high):
            z_stage(d)

    for d in range(1, n_ctx):
        origin = lax.rem(ctx + n_ctx - d, n_ctx)
        remote(stats.at[origin], stats.at[origin], st_s.at[d], st_r.at[d],
               layer, ctx).wait_recv()
    whole = stats[0]
    for j in range(1, n_ctx):
        whole = whole + stats[j]
    hg_ref[...] = whole[0:classes]
    loss_ref[0] = jnp.sum(whole[classes : classes + 1, 0:local]) * (1.0 / (local * n_ctx))

    result = mine[...]
    for d in range(n_high - 1):
        z_copy(d).wait_recv()
        result = result + recv_z[d].astype(jnp.float32)
    gk_ref[...] = result[0]
    gv_ref[...] = result[1]

    for d in range(1, n_high):
        line_copy(d).wait_send()
    for d in range(n_high - 1):
        z_copy(d).wait_send()
    for d in range(n_high):
        twin_copy(d, low).wait_send()
        x_copy(d).wait_send()
    for d in range(1, n_ctx):
        remote(stats.at[ctx], stats.at[ctx], st_s.at[d], st_r.at[d],
               layer, lax.rem(ctx + d, n_ctx)).wait_send()

    def sent_later(to, carry):
        remote(kv.at[ctx], kv.at[ctx], gc_s.at[to], gc_r.at[ctx], layer, to).wait_send()
        return carry

    lax.fori_loop(ctx + 1, split, sent_later, 0)

    def sent_half(to, carry):
        for d in range(n_high):
            half_copy(to, d).wait_send()
        return carry

    lax.fori_loop(split, end, sent_half, 0)

    def sent_back(j, carry):
        @pl.when(halved(j))
        def _():
            for d in range(n_high):
                forward_copy(j, d, low).wait_send()
                twin_half(j, d).wait_send()
                half_sum(j, d).wait_send()

        @pl.when(jnp.logical_not(halved(j)))
        def _():
            remote(send_ctx.at[j], recv_ctx.at[ctx], rc_s.at[j], rc_r.at[ctx, 0],
                   layer, j).wait_send()
        return carry

    lax.fori_loop(first, ctx, sent_back, 0)


def write_out(*refs):
    copies = [pltpu.make_async_copy(refs[i], refs[4 + i], refs[8].at[i]) for i in range(4)]
    for copy in copies:
        copy.start()
    for copy in copies:
        copy.wait()


def per_device(queries, keys, values, head, segments, label_mask, labels):
    n_layer, n_ctx = lax.axis_size("layer"), lax.axis_size("ctx")
    local, width = queries.shape[1:]
    rows, kv_width = keys.shape
    classes = head.shape[2]
    n_high = n_layer // 2
    G, W, T = KEY_VALUE_HEADS, HEAD_WIDTH, GROUP * local
    vmem = pl.BlockSpec(memory_space=pltpu.VMEM)
    bf, f32 = jnp.bfloat16, jnp.float32
    dma = pltpu.SemaphoreType.DMA
    results = ((local, width), (rows, kv_width), (rows, kv_width), (classes, width))
    results_bytes = 4 * sum(a * b for a, b in results)
    loss, *computed = pl.pallas_call(
        functools.partial(kernel, n_layer, n_ctx),
        out_shape=(
            jax.ShapeDtypeStruct((1,), f32),
            *(pltpu.VMEM(shape, f32) for shape in results),
        ),
        in_specs=[pl.BlockSpec(memory_space=pltpu.HBM)] * 7,
        out_specs=(pl.BlockSpec(memory_space=pltpu.SMEM), vmem, vmem, vmem, vmem),
        scratch_shapes=[
            pltpu.VMEM((local, width), bf),
            pltpu.VMEM((classes, width), f32),
            pltpu.VMEM((n_ctx, local), jnp.int32),
            pltpu.VMEM((1, local), jnp.int32),
            pltpu.VMEM((1, local), jnp.int32),
            dma((7,)),
            pltpu.VMEM((n_ctx, n_layer, 2, rows, kv_width), bf),
            pltpu.VMEM((n_ctx, G, local, T), f32),
            pltpu.VMEM((classes, QUERY_HEADS, W, local), f32),
            pltpu.VMEM((G, 1, T), f32),
            pltpu.VMEM((n_ctx, G, 1, T), f32),
            pltpu.VMEM((G, 1, T), f32),
            pltpu.VMEM((G, W, T), f32),
            pltpu.VMEM((G, W, T), bf),
            pltpu.VMEM((G, 1, T), f32),
            pltpu.VMEM((G, W, T), f32),
            pltpu.VMEM((n_layer, 2, rows, kv_width), f32),
            pltpu.VMEM((2, rows, kv_width), f32),
            pltpu.VMEM((STAT_ROWS, local), f32),
            pltpu.VMEM((n_ctx, STAT_ROWS, width), f32),
            pltpu.VMEM((n_ctx, n_layer, 2, rows, kv_width), bf),
            pltpu.VMEM((n_ctx, n_layer, 2, rows, kv_width), bf),
            pltpu.VMEM((n_high, 2, rows, kv_width), bf),
            pltpu.VMEM((n_high, 2, rows, kv_width), bf),
            pltpu.VMEM((n_high, 2, rows, kv_width), bf),
            pltpu.VMEM((n_high, 2, rows, kv_width), bf),
            *[pltpu.VMEM((n_ctx, n_high, 2, rows, kv_width), bf)] * 3,
            dma((n_high,)), dma((n_high,)), dma((n_high,)), dma((n_high,)),
            dma((n_ctx,)), dma((n_ctx,)), dma((n_ctx,)), dma((n_ctx,)),
            dma((n_ctx,)), dma((n_ctx, n_high)), dma((n_high,)), dma((n_high,)),
            dma((n_high,)), dma((n_high,)),
            *[dma((n_ctx, n_high))] * 8,
        ],
        compiler_params=pltpu.CompilerParams(
            collective_id=0, has_side_effects=True, vmem_limit_bytes=64 * 1024 * 1024 - results_bytes - 256 * 1024),
    )(
        queries[0], keys, values, jnp.swapaxes(head[0], 0, 1),
        segments.reshape(n_ctx, local), label_mask[None], labels[None],
    )
    hbm = pl.BlockSpec(memory_space=pltpu.HBM)
    dq, gk, gv, hg = pl.pallas_call(
        write_out,
        out_shape=tuple(jax.ShapeDtypeStruct(shape, f32) for shape in results),
        in_specs=[vmem] * 4,
        out_specs=(hbm,) * 4,
        scratch_shapes=[dma((4,))],
        compiler_params=pltpu.CompilerParams(vmem_limit_bytes=2 * results_bytes),
    )(*computed)
    return loss, dq[None], gk, gv, jnp.swapaxes(hg, 0, 1)[None]


def solution(mesh):
    return jax.shard_map(
        per_device,
        mesh=mesh,
        in_specs=(
            P("layer", "ctx", None),
            P(("ctx", "layer"), None),
            P(("ctx", "layer"), None),
            P("layer", None, None),
            P(),
            P("ctx"),
            P("ctx"),
        ),
        out_specs=(
            P("layer"),
            P("layer", "ctx", None),
            P(("ctx", "layer"), None),
            P(("ctx", "layer"), None),
            P("layer", None, None),
        ),
        check_vma=False,
    )
```

```python
import functools

import jax
import jax.numpy as jnp
from jax import lax
from jax.experimental import pallas as pl
from jax.experimental.pallas import tpu as pltpu
from jax.sharding import PartitionSpec as P

QUERY_HEADS = 12
KEY_VALUE_HEADS = 4
HEAD_WIDTH = 128

GROUP = QUERY_HEADS // KEY_VALUE_HEADS
LOG2_E = 1.4426950408889634
NEGATIVE_FILL = -1e30
HIGH = lax.Precision.HIGHEST
MESH = pl.DeviceIdType.MESH
STAT_ROWS = 8


def dot(a, b, a_dim, b_dim, precision=None):
    return lax.dot_general(
        a, b, (((a_dim,), (b_dim,)), ((), ())), precision=precision,
        preferred_element_type=jnp.float32,
    )


def kernel(
    n_layer, n_ctx, q_in, k_in, v_in, head_in, seg_in, mask_in, label_in,
    loss_ref, dq_ref, gk_ref, gv_ref, hg_ref,
    q_ref, head_ref, seg_ref, mask_ref, label_ref, in_sem,
    kv, score, hb, peak, tops, total, att, datt, delta, dqt, grad, mine, rows_d, stats,
    send_ctx, recv_ctx, send_x, recv_x, send_z, recv_z,
    gz_s, gz_r, gx_s, gx_r, gc_s, gc_r, st_s, st_r, rc_s, rc_r, rx_s, rx_r, rz_s, rz_r, rt_r,
):
    W = HEAD_WIDTH
    local = q_ref.shape[0]
    rows = k_in.shape[0]
    classes = head_ref.shape[0]
    n_high = n_layer // 2
    layer, ctx = lax.axis_index("layer"), lax.axis_index("ctx")
    high, low = layer // 2, layer % 2
    twin = high * 2 + (1 - low)
    tail = (3 * n_ctx) // 4
    in_tail = (ctx >= tail).astype(jnp.int32)
    first = in_tail * tail
    end = tail + in_tail * (n_ctx - tail)
    count = ctx - first + 1

    def remote(src, dst, s, r, to_layer, to_ctx):
        return pltpu.make_async_remote_copy(
            src_ref=src, dst_ref=dst, send_sem=s, recv_sem=r,
            device_id=(to_layer, to_ctx), device_id_type=MESH,
        )

    k_load, v_load, head_load, q_load, *small_loads = [
        pltpu.make_async_copy(src, dst, in_sem.at[i])
        for i, (src, dst) in enumerate([
            (k_in, kv.at[ctx, layer, 0]), (v_in, kv.at[ctx, layer, 1]), (head_in, head_ref),
            (q_in, q_ref), (seg_in, seg_ref), (mask_in, mask_ref), (label_in, label_ref)])
    ]
    for load in (k_load, v_load, head_load, q_load, *small_loads):
        load.start()

    barrier = pltpu.get_barrier_semaphore()
    for d in range(1, n_high):
        pl.semaphore_signal(
            barrier, inc=1, device_id=(lax.rem(high + d, n_high) * 2 + low, ctx),
            device_id_type=MESH)
    pl.semaphore_signal(barrier, inc=1, device_id=(twin, ctx), device_id_type=MESH)
    for d in range(1, n_ctx):
        for to_layer in (layer, twin):
            pl.semaphore_signal(
                barrier, inc=1, device_id=(to_layer, lax.rem(ctx + d, n_ctx)),
                device_id_type=MESH)
    k_load.wait()
    v_load.wait()
    pl.semaphore_wait(barrier, n_high + 2 * (n_ctx - 1))

    def to_later(piece):
        def one(to, carry):
            for to_layer in (layer, twin):
                remote(kv.at[ctx, piece], kv.at[ctx, piece], gc_s.at[to], gc_r.at[ctx],
                       to_layer, to).start()
            return carry
        lax.fori_loop(ctx + 1, end, one, 0)

    def line_copy(d):
        return remote(kv.at[ctx, layer], kv.at[ctx, layer], gz_s.at[d], gz_r.at[d],
                      lax.rem(high + d, n_high) * 2 + low, ctx)

    def twin_copy(d, side):
        piece = lax.rem(high + n_high - d, n_high) * 2 + side
        return remote(kv.at[ctx, piece], kv.at[ctx, piece], gx_s.at[d], gx_r.at[d], twin, ctx)

    for d in range(1, n_high):
        line_copy(d).start()
    twin_copy(0, low).start()
    to_later(layer)

    head_load.wait()
    for k in range(classes):
        for h in range(QUERY_HEADS):
            row = head_ref[k : k + 1, h * W : (h + 1) * W]
            hb[k, h] = jnp.transpose(jnp.broadcast_to(row, (local, W)))

    for d in range(1, n_high):
        piece = lax.rem(high + n_high - d, n_high) * 2 + low
        remote(kv.at[ctx, piece], kv.at[ctx, piece], gz_s.at[d], gz_r.at[d],
               layer, ctx).wait_recv()
        twin_copy(d, low).start()
        to_later(piece)
    for d in range(n_high):
        twin_copy(d, 1 - low).wait_recv()

    def block_of(j, which, g):
        part = kv[j, :, which, :, g * W : (g + 1) * W]
        if rows % 16:
            return part.astype(jnp.float32).reshape(n_layer * rows, W).astype(jnp.bfloat16)
        return part.reshape(n_layer * rows, W)

    def query_of(g):
        return jnp.concatenate(
            [q_ref[:, (g * GROUP + r) * W : (g * GROUP + r + 1) * W] for r in range(GROUP)], axis=0)

    peak[...] = jnp.full_like(peak, NEGATIVE_FILL)
    total[...] = jnp.zeros_like(total)
    att[...] = jnp.zeros_like(att)
    dqt[...] = jnp.zeros_like(dqt)

    for load in (q_load, *small_loads):
        load.wait()
    seg_q = seg_ref[pl.ds(ctx, 1), :]

    def score_block(i, carry):
        j = ctx - i

        if not isinstance(i, int):
            remote(kv.at[j], kv.at[j], gc_s.at[j], gc_r.at[j], layer, ctx).wait_recv()

        seg_k = jnp.transpose(
            jnp.broadcast_to(seg_ref[pl.ds(j, 1), :], (local, local)).astype(jnp.float32))
        same = seg_k == jnp.broadcast_to(seg_q, (local, local)).astype(jnp.float32)
        k_pos = j * local + lax.broadcasted_iota(jnp.int32, (local, local), 0)
        q_pos = ctx * local + lax.broadcasted_iota(jnp.int32, (local, local), 1)
        fill = jnp.where(same & (k_pos <= q_pos), 0.0, NEGATIVE_FILL)
        fill = jnp.concatenate([fill] * GROUP, axis=1)
        ahead = dot(block_of(j, 0, 0), query_of(0), 1, 1)
        for g in range(KEY_VALUE_HEADS):
            s = jnp.where(fill < 0.0, NEGATIVE_FILL, ahead * (LOG2_E * W ** -0.5))
            if g + 1 < KEY_VALUE_HEADS:
                ahead = dot(block_of(j, 0, g + 1), query_of(g + 1), 1, 1)
            top = jnp.maximum(peak[g], jnp.max(s, axis=0, keepdims=True))
            fade = jnp.exp2(peak[g] - top)
            p = jnp.exp2(s - top)
            score[j, g] = p
            tops[j, g] = top
            peak[g] = top
            total[g] = total[g] * fade + jnp.sum(p, axis=0, keepdims=True)
            att[g] = att[g] * fade + dot(block_of(j, 1, g), p.astype(jnp.bfloat16), 0, 0)
        return carry

    score_block(0, 0)

    lax.fori_loop(1, count, score_block, 0)

    logits = [jnp.zeros((1, local), jnp.float32) for _ in range(classes)]
    parts = []
    for g in range(KEY_VALUE_HEADS):
        inverse = 1.0 / total[g]
        total[g] = inverse
        att[g] = att[g] * inverse
        for r in range(GROUP):
            a = att[g, :, r * W : (r + 1) * W]
            part = [jnp.sum(hb[k, g * GROUP + r] * a, axis=0, keepdims=True)
                    for k in range(classes)]
            parts.append(part)
            logits = [x + y for x, y in zip(logits, part)]
    biggest = functools.reduce(jnp.maximum, logits)
    log_total = biggest + jnp.log(sum(jnp.exp(x - biggest) for x in logits))
    mask = mask_ref[...].astype(jnp.float32)
    hot = [(label_ref[...] == k).astype(jnp.float32) for k in range(classes)]
    loss_rows = mask * (log_total - sum(o * x for o, x in zip(hot, logits)))
    d_logits = [mask * (jnp.exp(x - log_total) - o) for o, x in zip(hot, logits)]

    for h in range(QUERY_HEADS):
        g, r = h // GROUP, h % GROUP
        cols = slice(r * W, (r + 1) * W)
        da = sum(hb[k, h] * d_logits[k] for k in range(classes))
        datt[g, :, cols] = da.astype(jnp.bfloat16)
        delta[g, :, cols] = sum(parts[h][k] * d_logits[k] for k in range(classes))
    for k in range(classes):
        rows_d[k : k + 1, :] = d_logits[k]
    rows_d[classes : classes + 1, :] = loss_rows

    def back_block(j, keep):
        ahead = dot(block_of(j, 1, 0), datt[0], 1, 0)
        for g in range(KEY_VALUE_HEADS):
            dp = ahead
            if g + 1 < KEY_VALUE_HEADS:
                ahead = dot(block_of(j, 1, g + 1), datt[g + 1], 1, 0)
            prob = score[j, g] * (total[g] * jnp.exp2(tops[j, g] - peak[g]))
            ds = (prob * ((dp - delta[g]) * W ** -0.5)).astype(jnp.bfloat16)
            cols = slice(g * W, (g + 1) * W)
            keep(1, cols, dot(prob.astype(jnp.bfloat16), datt[g], 1, 1))
            keep(0, cols, dot(ds, query_of(g), 1, 0))
            dqt[g] += dot(block_of(j, 0, g), ds, 0, 0)

    def place(d):
        return lax.rem(high + 1 + d, n_high)

    def earlier_block(j, carry):
        def keep(which, cols, value):
            send_ctx[j, :, which, :, cols] = value.reshape(n_layer, rows, W).astype(jnp.bfloat16)

        back_block(j, keep)
        for d in range(n_high):
            pair = place(d) * 2
            remote(send_ctx.at[j, pair + low], recv_ctx.at[ctx, pair + low], rc_s.at[j],
                   rc_r.at[ctx, d], layer, j).start()
            remote(send_ctx.at[j, pair + (1 - low)], recv_ctx.at[ctx, pair + low], rc_s.at[j],
                   rt_r.at[ctx, d], twin, j).start()
        return carry

    lax.fori_loop(first, ctx, earlier_block, 0)

    def keep_own(which, cols, value):
        grad[:, which, :, cols] = value.reshape(n_layer, rows, W)

    back_block(ctx, keep_own)

    def side_work():
        stacked = jnp.concatenate(
            [rows_d[0:classes, :], jnp.zeros((STAT_ROWS - classes, local), jnp.float32)], axis=0)
        for h in range(QUERY_HEADS):
            g, r = h // GROUP, h % GROUP
            stats[ctx, :, h * W : (h + 1) * W] = dot(
                stacked, att[g, :, r * W : (r + 1) * W], 1, 1, HIGH)
        stats[ctx, classes : classes + 1, 0:local] = rows_d[classes : classes + 1, :]
        for d in range(1, n_ctx):
            remote(stats.at[ctx], stats.at[ctx], st_s.at[d], st_r.at[d],
                   layer, lax.rem(ctx + d, n_ctx)).start()
        for h in range(QUERY_HEADS):
            g, r = h // GROUP, h % GROUP
            dq_ref[:, h * W : (h + 1) * W] = jnp.transpose(dqt[g, :, r * W : (r + 1) * W])

    def x_copy(d):
        return remote(send_x.at[d], recv_x.at[d], rx_s.at[d], rx_r.at[d], twin, ctx)

    def z_copy(d):
        return remote(send_z.at[d], recv_z.at[d], rz_s.at[d], rz_r.at[d],
                      place(d) * 2 + low, ctx)

    def x_stage(d):
        send_x[d] = grad[place(d) * 2 + (1 - low)].astype(jnp.bfloat16)
        x_copy(d).start()

    def z_stage(d):
        x_copy(d).wait_recv()
        pair = place(d) * 2
        own = pair + low
        grad[own] = grad[own] + recv_x[d].astype(jnp.float32)

        def one(i, carry):
            for side, arrived in ((low, rc_r), (1 - low, rt_r)):
                remote(send_ctx.at[i, pair + side], recv_ctx.at[i, pair + side], rc_s.at[i],
                       arrived.at[i, d], layer, ctx).wait_recv()
            grad[own] = grad[own] + (recv_ctx[i, own].astype(jnp.float32)
                                     + recv_ctx[i, pair + (1 - low)].astype(jnp.float32))
            return carry

        lax.fori_loop(ctx + 1, end, one, 0)
        value = grad[own]
        if d < n_high - 1:
            send_z[d] = value.astype(jnp.bfloat16)
            z_copy(d).start()
        else:
            mine[...] = value

    for d in range(n_high):
        x_stage(d)
    side_work()
    for d in range(n_high):
        z_stage(d)

    for d in range(1, n_ctx):
        origin = lax.rem(ctx + n_ctx - d, n_ctx)
        remote(stats.at[origin], stats.at[origin], st_s.at[d], st_r.at[d],
               layer, ctx).wait_recv()
    whole = stats[0]
    for j in range(1, n_ctx):
        whole = whole + stats[j]
    hg_ref[...] = whole[0:classes]
    loss_ref[0] = jnp.sum(whole[classes : classes + 1, 0:local]) * (1.0 / (local * n_ctx))

    result = mine[...]
    for d in range(n_high - 1):
        z_copy(d).wait_recv()
        result = result + recv_z[d].astype(jnp.float32)
    gk_ref[...] = result[0]
    gv_ref[...] = result[1]

    for d in range(1, n_high):
        line_copy(d).wait_send()
    for d in range(n_high - 1):
        z_copy(d).wait_send()
    for d in range(n_high):
        twin_copy(d, low).wait_send()
        x_copy(d).wait_send()
    for d in range(1, n_ctx):
        remote(stats.at[ctx], stats.at[ctx], st_s.at[d], st_r.at[d],
               layer, lax.rem(ctx + d, n_ctx)).wait_send()

    def sent_later(to, carry):
        remote(kv.at[ctx], kv.at[ctx], gc_s.at[to], gc_r.at[ctx], layer, to).wait_send()
        return carry

    lax.fori_loop(ctx + 1, end, sent_later, 0)

    def sent_back(j, carry):
        remote(send_ctx.at[j], recv_ctx.at[ctx], rc_s.at[j], rc_r.at[ctx, 0], layer, j).wait_send()
        return carry

    lax.fori_loop(first, ctx, sent_back, 0)


def write_out(*refs):
    copies = [pltpu.make_async_copy(refs[i], refs[4 + i], refs[8].at[i]) for i in range(4)]
    for copy in copies:
        copy.start()
    for copy in copies:
        copy.wait()


def per_device(queries, keys, values, head, segments, label_mask, labels):
    n_layer, n_ctx = lax.axis_size("layer"), lax.axis_size("ctx")
    local, width = queries.shape[1:]
    rows, kv_width = keys.shape
    classes = head.shape[2]
    n_high = n_layer // 2
    G, W, T = KEY_VALUE_HEADS, HEAD_WIDTH, GROUP * local
    vmem = pl.BlockSpec(memory_space=pltpu.VMEM)
    bf, f32 = jnp.bfloat16, jnp.float32
    dma = pltpu.SemaphoreType.DMA
    results = ((local, width), (rows, kv_width), (rows, kv_width), (classes, width))
    results_bytes = 4 * sum(a * b for a, b in results)
    loss, *computed = pl.pallas_call(
        functools.partial(kernel, n_layer, n_ctx),
        out_shape=(
            jax.ShapeDtypeStruct((1,), f32),
            *(pltpu.VMEM(shape, f32) for shape in results),
        ),
        in_specs=[pl.BlockSpec(memory_space=pltpu.HBM)] * 7,
        out_specs=(pl.BlockSpec(memory_space=pltpu.SMEM), vmem, vmem, vmem, vmem),
        scratch_shapes=[
            pltpu.VMEM((local, width), bf),
            pltpu.VMEM((classes, width), f32),
            pltpu.VMEM((n_ctx, local), jnp.int32),
            pltpu.VMEM((1, local), jnp.int32),
            pltpu.VMEM((1, local), jnp.int32),
            dma((7,)),
            pltpu.VMEM((n_ctx, n_layer, 2, rows, kv_width), bf),
            pltpu.VMEM((n_ctx, G, local, T), f32),
            pltpu.VMEM((classes, QUERY_HEADS, W, local), f32),
            pltpu.VMEM((G, 1, T), f32),
            pltpu.VMEM((n_ctx, G, 1, T), f32),
            pltpu.VMEM((G, 1, T), f32),
            pltpu.VMEM((G, W, T), f32),
            pltpu.VMEM((G, W, T), bf),
            pltpu.VMEM((G, 1, T), f32),
            pltpu.VMEM((G, W, T), f32),
            pltpu.VMEM((n_layer, 2, rows, kv_width), f32),
            pltpu.VMEM((2, rows, kv_width), f32),
            pltpu.VMEM((STAT_ROWS, local), f32),
            pltpu.VMEM((n_ctx, STAT_ROWS, width), f32),
            pltpu.VMEM((n_ctx, n_layer, 2, rows, kv_width), bf),
            pltpu.VMEM((n_ctx, n_layer, 2, rows, kv_width), bf),
            pltpu.VMEM((n_high, 2, rows, kv_width), bf),
            pltpu.VMEM((n_high, 2, rows, kv_width), bf),
            pltpu.VMEM((n_high, 2, rows, kv_width), bf),
            pltpu.VMEM((n_high, 2, rows, kv_width), bf),
            dma((n_high,)), dma((n_high,)), dma((n_high,)), dma((n_high,)),
            dma((n_ctx,)), dma((n_ctx,)), dma((n_ctx,)), dma((n_ctx,)),
            dma((n_ctx,)), dma((n_ctx, n_high)), dma((n_high,)), dma((n_high,)),
            dma((n_high,)), dma((n_high,)), dma((n_ctx, n_high)),
        ],
        compiler_params=pltpu.CompilerParams(
            collective_id=0, has_side_effects=True, vmem_limit_bytes=64 * 1024 * 1024 - results_bytes - 256 * 1024),
    )(
        queries[0], keys, values, jnp.swapaxes(head[0], 0, 1),
        segments.reshape(n_ctx, local), label_mask[None], labels[None],
    )
    hbm = pl.BlockSpec(memory_space=pltpu.HBM)
    dq, gk, gv, hg = pl.pallas_call(
        write_out,
        out_shape=tuple(jax.ShapeDtypeStruct(shape, f32) for shape in results),
        in_specs=[vmem] * 4,
        out_specs=(hbm,) * 4,
        scratch_shapes=[dma((4,))],
        compiler_params=pltpu.CompilerParams(vmem_limit_bytes=2 * results_bytes),
    )(*computed)
    return loss, dq[None], gk, gv, jnp.swapaxes(hg, 0, 1)[None]


def solution(mesh):
    return jax.shard_map(
        per_device,
        mesh=mesh,
        in_specs=(
            P("layer", "ctx", None),
            P(("ctx", "layer"), None),
            P(("ctx", "layer"), None),
            P("layer", None, None),
            P(),
            P("ctx"),
            P("ctx"),
        ),
        out_specs=(
            P("layer"),
            P("layer", "ctx", None),
            P(("ctx", "layer"), None),
            P(("ctx", "layer"), None),
            P("layer", None, None),
        ),
        check_vma=False,
    )
```

```python
import functools

import jax
import jax.numpy as jnp
from jax import lax
from jax.experimental import pallas as pl
from jax.experimental.pallas import tpu as pltpu
from jax.sharding import PartitionSpec as P

QUERY_HEADS = 12
KEY_VALUE_HEADS = 4
HEAD_WIDTH = 128

GROUP = QUERY_HEADS // KEY_VALUE_HEADS
LOG2_E = 1.4426950408889634
NEGATIVE_FILL = -1e30
HIGH = lax.Precision.HIGHEST
MESH = pl.DeviceIdType.MESH
STAT_ROWS = 8


def dot(a, b, a_dim, b_dim, precision=None):
    return lax.dot_general(
        a, b, (((a_dim,), (b_dim,)), ((), ())), precision=precision,
        preferred_element_type=jnp.float32,
    )


def kernel(
    n_layer, n_ctx, q_in, k_in, v_in, head_in, seg_in, mask_in, label_in,
    loss_ref, dq_ref, gk_ref, gv_ref, hg_ref,
    q_ref, head_ref, seg_ref, mask_ref, label_ref, in_sem,
    kv, score, hb, peak, tops, total, att, datt, delta, dqt, scores16, grad, mine, rows_d, stats,
    send_ctx, recv_ctx, send_x, recv_x, send_z, recv_z,
    gz_s, gz_r, gx_s, gx_r, gc_s, gc_r, st_s, st_r, rc_s, rc_r, rx_s, rx_r, rz_s, rz_r, rt_r,
):
    W = HEAD_WIDTH
    local = q_ref.shape[0]
    rows = k_in.shape[0]
    classes = head_ref.shape[0]
    n_high = n_layer // 2
    layer, ctx = lax.axis_index("layer"), lax.axis_index("ctx")
    high, low = layer // 2, layer % 2
    twin = high * 2 + (1 - low)
    tail = (3 * n_ctx) // 4
    in_tail = (ctx >= tail).astype(jnp.int32)
    first = in_tail * tail
    end = tail + in_tail * (n_ctx - tail)
    count = ctx - first + 1

    def remote(src, dst, s, r, to_layer, to_ctx):
        return pltpu.make_async_remote_copy(
            src_ref=src, dst_ref=dst, send_sem=s, recv_sem=r,
            device_id=(to_layer, to_ctx), device_id_type=MESH,
        )

    k_load, v_load, head_load, q_load, *small_loads = [
        pltpu.make_async_copy(src, dst, in_sem.at[i])
        for i, (src, dst) in enumerate([
            (k_in, kv.at[ctx, layer, 0]), (v_in, kv.at[ctx, layer, 1]), (head_in, head_ref),
            (q_in, q_ref), (seg_in, seg_ref), (mask_in, mask_ref), (label_in, label_ref)])
    ]
    for load in (k_load, v_load, head_load, q_load, *small_loads):
        load.start()

    barrier = pltpu.get_barrier_semaphore()
    for d in range(1, n_high):
        pl.semaphore_signal(
            barrier, inc=1, device_id=(lax.rem(high + d, n_high) * 2 + low, ctx),
            device_id_type=MESH)
    pl.semaphore_signal(barrier, inc=1, device_id=(twin, ctx), device_id_type=MESH)
    for d in range(1, n_ctx):
        for to_layer in (layer, twin):
            pl.semaphore_signal(
                barrier, inc=1, device_id=(to_layer, lax.rem(ctx + d, n_ctx)),
                device_id_type=MESH)
    k_load.wait()
    v_load.wait()
    pl.semaphore_wait(barrier, n_high + 2 * (n_ctx - 1))

    def to_later(piece):
        def one(to, carry):
            for to_layer in (layer, twin):
                remote(kv.at[ctx, piece], kv.at[ctx, piece], gc_s.at[to], gc_r.at[ctx],
                       to_layer, to).start()
            return carry
        lax.fori_loop(ctx + 1, end, one, 0)

    def line_copy(d):
        return remote(kv.at[ctx, layer], kv.at[ctx, layer], gz_s.at[d], gz_r.at[d],
                      lax.rem(high + d, n_high) * 2 + low, ctx)

    def twin_copy(d, side):
        piece = lax.rem(high + n_high - d, n_high) * 2 + side
        return remote(kv.at[ctx, piece], kv.at[ctx, piece], gx_s.at[d], gx_r.at[d], twin, ctx)

    for d in range(1, n_high):
        line_copy(d).start()
    twin_copy(0, low).start()
    to_later(layer)

    head_load.wait()
    for k in range(classes):
        for h in range(QUERY_HEADS):
            row = head_ref[k : k + 1, h * W : (h + 1) * W]
            hb[k, h] = jnp.transpose(jnp.broadcast_to(row, (local, W)))

    for d in range(1, n_high):
        piece = lax.rem(high + n_high - d, n_high) * 2 + low
        remote(kv.at[ctx, piece], kv.at[ctx, piece], gz_s.at[d], gz_r.at[d],
               layer, ctx).wait_recv()
        twin_copy(d, low).start()
        to_later(piece)
    for d in range(n_high):
        twin_copy(d, 1 - low).wait_recv()

    def block_of(j, which, g):
        part = kv[j, :, which, :, g * W : (g + 1) * W]
        if rows % 16:
            return part.astype(jnp.float32).reshape(n_layer * rows, W).astype(jnp.bfloat16)
        return part.reshape(n_layer * rows, W)

    def query_of(g):
        return jnp.concatenate(
            [q_ref[:, (g * GROUP + r) * W : (g * GROUP + r + 1) * W] for r in range(GROUP)], axis=0)

    peak[...] = jnp.full_like(peak, NEGATIVE_FILL)
    total[...] = jnp.zeros_like(total)
    att[...] = jnp.zeros_like(att)
    dqt[...] = jnp.zeros_like(dqt)

    for load in (q_load, *small_loads):
        load.wait()
    seg_q = seg_ref[pl.ds(ctx, 1), :]

    def score_block(i, carry):
        j = ctx - i

        if not isinstance(i, int):
            remote(kv.at[j], kv.at[j], gc_s.at[j], gc_r.at[j], layer, ctx).wait_recv()

        seg_k = jnp.transpose(
            jnp.broadcast_to(seg_ref[pl.ds(j, 1), :], (local, local)).astype(jnp.float32))
        same = seg_k == jnp.broadcast_to(seg_q, (local, local)).astype(jnp.float32)
        k_pos = j * local + lax.broadcasted_iota(jnp.int32, (local, local), 0)
        q_pos = ctx * local + lax.broadcasted_iota(jnp.int32, (local, local), 1)
        fill = jnp.where(same & (k_pos <= q_pos), 0.0, NEGATIVE_FILL)
        fill = jnp.concatenate([fill] * GROUP, axis=1)
        ahead = dot(block_of(j, 0, 0), query_of(0), 1, 1)
        for g in range(KEY_VALUE_HEADS):
            s = jnp.where(fill < 0.0, NEGATIVE_FILL, ahead * (LOG2_E * W ** -0.5))
            if g + 1 < KEY_VALUE_HEADS:
                ahead = dot(block_of(j, 0, g + 1), query_of(g + 1), 1, 1)
            top = jnp.maximum(peak[g], jnp.max(s, axis=0, keepdims=True))
            fade = jnp.exp2(peak[g] - top)
            p = jnp.exp2(s - top)
            score[j, g] = p
            tops[j, g] = top
            peak[g] = top
            total[g] = total[g] * fade + jnp.sum(p, axis=0, keepdims=True)
            att[g] = att[g] * fade + dot(block_of(j, 1, g), p.astype(jnp.bfloat16), 0, 0)
        return carry

    score_block(0, 0)

    lax.fori_loop(1, count, score_block, 0)

    logits = [jnp.zeros((1, local), jnp.float32) for _ in range(classes)]
    parts = []
    for g in range(KEY_VALUE_HEADS):
        inverse = 1.0 / total[g]
        total[g] = inverse
        att[g] = att[g] * inverse
        for r in range(GROUP):
            a = att[g, :, r * W : (r + 1) * W]
            part = [jnp.sum(hb[k, g * GROUP + r] * a, axis=0, keepdims=True)
                    for k in range(classes)]
            parts.append(part)
            logits = [x + y for x, y in zip(logits, part)]
    biggest = functools.reduce(jnp.maximum, logits)
    log_total = biggest + jnp.log(sum(jnp.exp(x - biggest) for x in logits))
    mask = mask_ref[...].astype(jnp.float32)
    hot = [(label_ref[...] == k).astype(jnp.float32) for k in range(classes)]
    loss_rows = mask * (log_total - sum(o * x for o, x in zip(hot, logits)))
    d_logits = [mask * (jnp.exp(x - log_total) - o) for o, x in zip(hot, logits)]

    for h in range(QUERY_HEADS):
        g, r = h // GROUP, h % GROUP
        cols = slice(r * W, (r + 1) * W)
        da = sum(hb[k, h] * d_logits[k] for k in range(classes))
        datt[g, :, cols] = da.astype(jnp.bfloat16)
        delta[g, :, cols] = sum(parts[h][k] * d_logits[k] for k in range(classes))
    for k in range(classes):
        rows_d[k : k + 1, :] = d_logits[k]
    rows_d[classes : classes + 1, :] = loss_rows

    def back_block(j, keep):
        ahead = dot(block_of(j, 1, 0), datt[0], 1, 0)
        for g in range(KEY_VALUE_HEADS):
            dp = ahead
            if g + 1 < KEY_VALUE_HEADS:
                ahead = dot(block_of(j, 1, g + 1), datt[g + 1], 1, 0)
            prob = score[j, g] * (total[g] * jnp.exp2(tops[j, g] - peak[g]))
            ds = (prob * ((dp - delta[g]) * W ** -0.5)).astype(jnp.bfloat16)
            cols = slice(g * W, (g + 1) * W)
            keep(1, cols, dot(prob.astype(jnp.bfloat16), datt[g], 1, 1))
            keep(0, cols, dot(ds, query_of(g), 1, 0))
            scores16[j, g] = ds

    def place(d):
        return lax.rem(high + 1 + d, n_high)

    def earlier_block(j, carry):
        def keep(which, cols, value):
            send_ctx[j, :, which, :, cols] = value.reshape(n_layer, rows, W).astype(jnp.bfloat16)

        back_block(j, keep)
        for d in range(n_high):
            pair = place(d) * 2
            remote(send_ctx.at[j, pair + low], recv_ctx.at[ctx, pair + low], rc_s.at[j],
                   rc_r.at[ctx, d], layer, j).start()
            remote(send_ctx.at[j, pair + (1 - low)], recv_ctx.at[ctx, pair + low], rc_s.at[j],
                   rt_r.at[ctx, d], twin, j).start()
        return carry

    lax.fori_loop(first, ctx, earlier_block, 0)

    def keep_own(which, cols, value):
        grad[:, which, :, cols] = value.reshape(n_layer, rows, W)

    back_block(ctx, keep_own)

    def side_work():
        stacked = jnp.concatenate(
            [rows_d[0:classes, :], jnp.zeros((STAT_ROWS - classes, local), jnp.float32)], axis=0)
        for h in range(QUERY_HEADS):
            g, r = h // GROUP, h % GROUP
            stats[ctx, :, h * W : (h + 1) * W] = dot(
                stacked, att[g, :, r * W : (r + 1) * W], 1, 1, HIGH)
        stats[ctx, classes : classes + 1, 0:local] = rows_d[classes : classes + 1, :]
        for d in range(1, n_ctx):
            remote(stats.at[ctx], stats.at[ctx], st_s.at[d], st_r.at[d],
                   layer, lax.rem(ctx + d, n_ctx)).start()

    def query_block(i, carry):
        j = first + i
        for g in range(KEY_VALUE_HEADS):
            dqt[g] += dot(block_of(j, 0, g), scores16[j, g], 0, 0)
        return carry

    def query_out():
        for h in range(QUERY_HEADS):
            g, r = h // GROUP, h % GROUP
            dq_ref[:, h * W : (h + 1) * W] = jnp.transpose(dqt[g, :, r * W : (r + 1) * W])

    def x_copy(d):
        return remote(send_x.at[d], recv_x.at[d], rx_s.at[d], rx_r.at[d], twin, ctx)

    def z_copy(d):
        return remote(send_z.at[d], recv_z.at[d], rz_s.at[d], rz_r.at[d],
                      place(d) * 2 + low, ctx)

    def x_stage(d):
        send_x[d] = grad[place(d) * 2 + (1 - low)].astype(jnp.bfloat16)
        x_copy(d).start()

    def z_stage(d):
        x_copy(d).wait_recv()
        pair = place(d) * 2
        own = pair + low
        grad[own] = grad[own] + recv_x[d].astype(jnp.float32)

        def one(i, carry):
            for side, arrived in ((low, rc_r), (1 - low, rt_r)):
                remote(send_ctx.at[i, pair + side], recv_ctx.at[i, pair + side], rc_s.at[i],
                       arrived.at[i, d], layer, ctx).wait_recv()
            grad[own] = grad[own] + (recv_ctx[i, own].astype(jnp.float32)
                                     + recv_ctx[i, pair + (1 - low)].astype(jnp.float32))
            return carry

        lax.fori_loop(ctx + 1, end, one, 0)
        value = grad[own]
        if d < n_high - 1:
            send_z[d] = value.astype(jnp.bfloat16)
            z_copy(d).start()
        else:
            mine[...] = value

    for d in range(n_high):
        x_stage(d)
    lax.fori_loop(0, count, query_block, 0)
    side_work()

    @pl.when(ctx < end - 1)
    def _():
        query_out()

    for d in range(n_high):
        z_stage(d)

    @pl.when(ctx == end - 1)
    def _():
        query_out()


    for d in range(1, n_ctx):
        origin = lax.rem(ctx + n_ctx - d, n_ctx)
        remote(stats.at[origin], stats.at[origin], st_s.at[d], st_r.at[d],
               layer, ctx).wait_recv()
    whole = stats[0]
    for j in range(1, n_ctx):
        whole = whole + stats[j]
    hg_ref[...] = whole[0:classes]
    loss_ref[0] = jnp.sum(whole[classes : classes + 1, 0:local]) * (1.0 / (local * n_ctx))

    result = mine[...]
    for d in range(n_high - 1):
        z_copy(d).wait_recv()
        result = result + recv_z[d].astype(jnp.float32)
    gk_ref[...] = result[0]
    gv_ref[...] = result[1]

    for d in range(1, n_high):
        line_copy(d).wait_send()
    for d in range(n_high - 1):
        z_copy(d).wait_send()
    for d in range(n_high):
        twin_copy(d, low).wait_send()
        x_copy(d).wait_send()
    for d in range(1, n_ctx):
        remote(stats.at[ctx], stats.at[ctx], st_s.at[d], st_r.at[d],
               layer, lax.rem(ctx + d, n_ctx)).wait_send()

    def sent_later(to, carry):
        remote(kv.at[ctx], kv.at[ctx], gc_s.at[to], gc_r.at[ctx], layer, to).wait_send()
        return carry

    lax.fori_loop(ctx + 1, end, sent_later, 0)

    def sent_back(j, carry):
        remote(send_ctx.at[j], recv_ctx.at[ctx], rc_s.at[j], rc_r.at[ctx, 0], layer, j).wait_send()
        return carry

    lax.fori_loop(first, ctx, sent_back, 0)


def write_out(*refs):
    copies = [pltpu.make_async_copy(refs[i], refs[4 + i], refs[8].at[i]) for i in range(4)]
    for copy in copies:
        copy.start()
    for copy in copies:
        copy.wait()


def per_device(queries, keys, values, head, segments, label_mask, labels):
    n_layer, n_ctx = lax.axis_size("layer"), lax.axis_size("ctx")
    local, width = queries.shape[1:]
    rows, kv_width = keys.shape
    classes = head.shape[2]
    n_high = n_layer // 2
    G, W, T = KEY_VALUE_HEADS, HEAD_WIDTH, GROUP * local
    vmem = pl.BlockSpec(memory_space=pltpu.VMEM)
    bf, f32 = jnp.bfloat16, jnp.float32
    dma = pltpu.SemaphoreType.DMA
    results = ((local, width), (rows, kv_width), (rows, kv_width), (classes, width))
    results_bytes = 4 * sum(a * b for a, b in results)
    loss, *computed = pl.pallas_call(
        functools.partial(kernel, n_layer, n_ctx),
        out_shape=(
            jax.ShapeDtypeStruct((1,), f32),
            *(pltpu.VMEM(shape, f32) for shape in results),
        ),
        in_specs=[pl.BlockSpec(memory_space=pltpu.HBM)] * 7,
        out_specs=(pl.BlockSpec(memory_space=pltpu.SMEM), vmem, vmem, vmem, vmem),
        scratch_shapes=[
            pltpu.VMEM((local, width), bf),
            pltpu.VMEM((classes, width), f32),
            pltpu.VMEM((n_ctx, local), jnp.int32),
            pltpu.VMEM((1, local), jnp.int32),
            pltpu.VMEM((1, local), jnp.int32),
            dma((7,)),
            pltpu.VMEM((n_ctx, n_layer, 2, rows, kv_width), bf),
            pltpu.VMEM((n_ctx, G, local, T), f32),
            pltpu.VMEM((classes, QUERY_HEADS, W, local), f32),
            pltpu.VMEM((G, 1, T), f32),
            pltpu.VMEM((n_ctx, G, 1, T), f32),
            pltpu.VMEM((G, 1, T), f32),
            pltpu.VMEM((G, W, T), f32),
            pltpu.VMEM((G, W, T), bf),
            pltpu.VMEM((G, 1, T), f32),
            pltpu.VMEM((G, W, T), f32),
            pltpu.VMEM((n_ctx, G, local, T), bf),
            pltpu.VMEM((n_layer, 2, rows, kv_width), f32),
            pltpu.VMEM((2, rows, kv_width), f32),
            pltpu.VMEM((STAT_ROWS, local), f32),
            pltpu.VMEM((n_ctx, STAT_ROWS, width), f32),
            pltpu.VMEM((n_ctx, n_layer, 2, rows, kv_width), bf),
            pltpu.VMEM((n_ctx, n_layer, 2, rows, kv_width), bf),
            pltpu.VMEM((n_high, 2, rows, kv_width), bf),
            pltpu.VMEM((n_high, 2, rows, kv_width), bf),
            pltpu.VMEM((n_high, 2, rows, kv_width), bf),
            pltpu.VMEM((n_high, 2, rows, kv_width), bf),
            dma((n_high,)), dma((n_high,)), dma((n_high,)), dma((n_high,)),
            dma((n_ctx,)), dma((n_ctx,)), dma((n_ctx,)), dma((n_ctx,)),
            dma((n_ctx,)), dma((n_ctx, n_high)), dma((n_high,)), dma((n_high,)),
            dma((n_high,)), dma((n_high,)), dma((n_ctx, n_high)),
        ],
        compiler_params=pltpu.CompilerParams(
            collective_id=0, has_side_effects=True, vmem_limit_bytes=64 * 1024 * 1024 - results_bytes - 256 * 1024),
    )(
        queries[0], keys, values, jnp.swapaxes(head[0], 0, 1),
        segments.reshape(n_ctx, local), label_mask[None], labels[None],
    )
    hbm = pl.BlockSpec(memory_space=pltpu.HBM)
    dq, gk, gv, hg = pl.pallas_call(
        write_out,
        out_shape=tuple(jax.ShapeDtypeStruct(shape, f32) for shape in results),
        in_specs=[vmem] * 4,
        out_specs=(hbm,) * 4,
        scratch_shapes=[dma((4,))],
        compiler_params=pltpu.CompilerParams(vmem_limit_bytes=2 * results_bytes),
    )(*computed)
    return loss, dq[None], gk, gv, jnp.swapaxes(hg, 0, 1)[None]


def solution(mesh):
    return jax.shard_map(
        per_device,
        mesh=mesh,
        in_specs=(
            P("layer", "ctx", None),
            P(("ctx", "layer"), None),
            P(("ctx", "layer"), None),
            P("layer", None, None),
            P(),
            P("ctx"),
            P("ctx"),
        ),
        out_specs=(
            P("layer"),
            P("layer", "ctx", None),
            P(("ctx", "layer"), None),
            P(("ctx", "layer"), None),
            P("layer", None, None),
        ),
        check_vma=False,
    )
```
